32 devices in a mesh: ctx: 16 (over z, y, core), seq: 2 (over x).
Axes of the slice: x: 2, y: 2, z: 4, core: 2. Of those that a mesh axis runs over, the one named last changes fastest.
Arguments:
- inputs: bfloat16 [4, 8192, 768], P('seq', 'ctx'), may hold values from -6 to 6
- out_grad: bfloat16 [4, 8192, 768], P('seq', 'ctx'), may hold values from -6 to 6
- segments: int32 [4, 8192], P('seq'), may hold values from 0 to 15, never falling along the last dimension, each value on 1 to 2048 neighbouring positions
- windows: int32 [12], replicated, may hold values from 256 to 1024, as said below
- owners: int32 [16], replicated, may hold values from 0 to 1, as said below
- weights: float32 [18, 768, 768], P('seq', 'ctx'), as said below
- first_moments: float32 [18, 768, 768], P('seq', 'ctx'), may hold values from -543.058 to 543.058
- second_moments: float32 [18, 768, 768], P('seq', 'ctx'), may hold values from 1966.08 to 32768
- norm_params: float32 [4, 768], replicated
- norm_first: float32 [4, 768], replicated, may hold values from -543.058 to 543.058
- norm_second: float32 [4, 768], replicated, may hold values from 1966.08 to 32768
Outputs:
- output: bfloat16 [4, 8192, 768], P('seq', 'ctx')
- input_grad: float32 [4, 8192, 768], P('seq', 'ctx')
- weight_grads: float32 [18, 768, 768], P('seq', 'ctx')
- norm_grads: float32 [4, 768], replicated
- new_weights: float32 [18, 768, 768], P('seq', 'ctx')
- new_first: float32 [18, 768, 768], P('seq', 'ctx')
- new_second: float32 [18, 768, 768], P('seq', 'ctx')
- weights_low: bfloat16 [18, 768, 768], P('seq', 'ctx')
- new_norms: float32 [4, 768], replicated
- new_norm_first: float32 [4, 768], replicated
- new_norm_second: float32 [4, 768], replicated
- factors: float32 [12], replicated
The draws below stay inside these ranges and needn't reach their ends.
Inputs may be any that keep to these rules, and one draw needn't show every extreme that they name: `segments`: segment numbers never fall along a sequence; a document holds at most a quarter of 8192 tokens. `windows`: some head has a window of exactly 1024. `owners`: each index of seq owns 1 to 9 units, and some index owns exactly 9. `weights`: slots that no unit occupies hold values that no output reads.
All inputs are finite; a program needn't handle non-finite values.
Results may differ from the reference program's by a relative error of at most 0.024.
Values may be sent and summed in bfloat16 or wider, within the bound.
No kernel may reach another device: no remote copies, remote signals or barrier semaphores. Data moves between devices by JAX's collectives and lax.ppermute only.
A program may use at most 320 MiB of HBM per device.

```python
import math
import jax
import jax.numpy as jnp
import numpy as np
from jax import lax

D = 768
HEADS = 12
HEAD_DIM = 64
FF = 3072
SEQ_LEN = 8192
WIN = 1024
STEP = 3
UNITS = 16
SLOTS = 9
SEQS = 4
TOKENS = 32768
N_SEQ = 2


def owner_list(key):
    base = jax.random.fold_in(key, 11)
    order = jax.random.permutation(jax.random.fold_in(base, 1), UNITS)
    offset = jax.random.randint(jax.random.fold_in(base, 2), (), 0, N_SEQ)
    place = jnp.arange(UNITS, dtype=jnp.int32)
    if UNITS % N_SEQ == 0:
        place = jnp.where(place == 0, 1, place)
    by_place = ((place + offset) % N_SEQ).astype(jnp.int32)
    return jnp.zeros((UNITS,), jnp.int32).at[order].set(by_place)


def draw_owners(key, part):
    return owner_list(key)


def draw_windows(key, part):
    widths = jax.random.randint(jax.random.fold_in(key, 21), (HEADS,), WIN // 4, WIN + 1)
    chosen = jax.random.randint(jax.random.fold_in(key, 22), (), 0, HEADS)
    return jnp.where(jnp.arange(HEADS) == chosen, WIN, widths).astype(jnp.int32)


def draw_weights(key, part):
    owners = owner_list(key)
    unit_ids = jnp.arange(UNITS, dtype=jnp.int32)
    same_owner = owners[None, :] == owners[:, None]
    earlier = unit_ids[None, :] < unit_ids[:, None]
    rank = jnp.sum((same_owner & earlier).astype(jnp.int32), axis=1)
    index = owners * SLOTS + rank
    slot_ids = jnp.arange(N_SEQ * SLOTS, dtype=jnp.int32)
    match = index[None, :] == slot_ids[:, None]
    groups = FF // D
    unit_scale = jnp.where(unit_ids == 3, 6.0 * D ** (-0.5), jnp.where(unit_ids >= 4 + 2 * groups, FF ** (-0.5), D ** (-0.5))).astype(jnp.float32)
    slot_scale = jnp.where(jnp.any(match, axis=1), jnp.sum(jnp.where(match, unit_scale[None, :], 0.0), axis=1), D ** (-0.5))
    head_scale = jnp.exp(jax.random.uniform(jax.random.fold_in(key, 13), (HEADS,), jnp.float32, 0.0, 1.0986))
    column_scale = jnp.repeat(head_scale, HEAD_DIM)
    factor = jnp.where(match[:, 0][:, None], column_scale[None, :], 1.0)
    shape = (N_SEQ * SLOTS, D, D)
    noise = jax.random.normal(jax.random.fold_in(key, 14), shape, jnp.float32)
    return (noise * slot_scale[:, None, None] * factor[:, None, :]).astype(jnp.float32)


def draw_norm_params(key, part):
    noise = jax.random.normal(jax.random.fold_in(key, 31), (4, D), jnp.float32)
    gains = (jnp.arange(4) % 2 == 0)[:, None]
    return jnp.where(gains, 1.0 + 0.1 * noise, 0.3 * noise).astype(jnp.float32)


def shard_levels(stream_key, shape, shards, low, largest):
    def one(dim, parts):
        draws = jax.random.uniform(jax.random.fold_in(jax.random.fold_in(stream_key, 6), dim), (parts,), jnp.float32, low / len(shards), largest / len(shards))
        return jnp.repeat(jnp.exp(draws), shape[dim] // parts).reshape((-1,) + (1,) * (len(shape) - dim - 1))

    factor_of = one(*shards[0])
    for cut in shards[1:]:
        factor_of = factor_of * one(*cut)
    return factor_of


def length_profile(count, total, limit, slope):
    portions = [(1 << 20) // math.isqrt(standing ** slope) + 1 for standing in range(2, count + 1)]
    spare, holding = total - limit - (count - 1), [1] * (count - 1)
    while spare > 0:
        movable = [i for i in range(count - 1) if holding[i] < limit]
        whole, remaining = sum([portions[i] for i in movable]), spare
        for i in movable:
            extra = min(limit - holding[i], max(1, remaining * portions[i] // whole), spare)
            holding[i] = holding[i] + extra
            spare = spare - extra
    return np.array([limit] + holding)


def ragged(own_key, number_of, total, limit, slope):
    if number_of == 2:
        one = jax.random.randint(own_key, (), max(1, total - limit), min(limit, total - 1) + 1)
        return jnp.stack([one, total - one])
    lengths = jnp.asarray(length_profile(number_of, total, limit, slope), jnp.int32)
    twos = (number_of - 1) // 2
    donor, receiver = lengths[1:1 + 2 * twos:2], lengths[2:2 + 2 * twos:2]
    room = jnp.minimum(donor - 1, limit - receiver)
    shifted = jax.random.randint(jax.random.fold_in(own_key, 1), (twos,), 0, 1 << 20) % (room + 1)
    lengths = lengths.at[1:1 + 2 * twos:2].set(donor - shifted).at[2:2 + 2 * twos:2].set(receiver + shifted)
    return lengths[jax.random.permutation(jax.random.fold_in(own_key, 2), number_of)]


def gaussian(stream_key, dims, deviation, limit, cuts=(), held_as=jnp.bfloat16):
    values = jax.random.normal(stream_key, dims, jnp.float32) * deviation
    if len(cuts) > 0:
        values = shard_levels(stream_key, dims, cuts, -0.22, 0.18) * values
    return jnp.clip(values, min=-limit, max=limit).astype(held_as)


def setup_inputs(seed: int = 0) -> dict:
    key_list = jax.random.split(jax.random.key(seed), 12)
    inputs = gaussian(key_list[0], (SEQS, SEQ_LEN, D), 1.0, 6.0, ((0, 2), (1, 16)))
    out_grad = gaussian(key_list[1], (SEQS, SEQ_LEN, D), 1.0, 6.0, ((0, 2), (1, 16)))
    segments = jax.vmap(lambda own: jnp.searchsorted(jnp.cumsum(ragged(own, 16, SEQ_LEN, SEQ_LEN // 4, 2)), jnp.arange(SEQ_LEN), side="right"))(jax.random.split(key_list[2], SEQS)).reshape((SEQS, SEQ_LEN)).astype(jnp.int32)
    windows = draw_windows(jax.random.fold_in(key_list[11], 71), 0)
    owners = draw_owners(jax.random.fold_in(key_list[11], 71), 0)
    weights = draw_weights(jax.random.fold_in(key_list[11], 71), 0)
    first_moments = gaussian(key_list[6], (N_SEQ * SLOTS, D, D), (0.5 * TOKENS ** 0.5), 543.058, ((0, 2), (1, 16)), jnp.float32)
    second_moments = jnp.clip(jnp.exp(math.log(32768.0) - 2.8134107 * jax.random.uniform(key_list[7], (N_SEQ * SLOTS, D, D), jnp.float32) ** shard_levels(key_list[7], (N_SEQ * SLOTS, D, D), ((0, 2), (1, 16)), -0.2, 0.2)), 1966.08, 32768.0)
    norm_params = draw_norm_params(jax.random.fold_in(key_list[11], 71), 0)
    norm_first = gaussian(key_list[9], (4, D), (0.5 * TOKENS ** 0.5), 543.058, (), jnp.float32)
    norm_second = jnp.clip(jnp.exp(jax.random.uniform(key_list[10], (4, D), jnp.float32, math.log(1966.08), math.log(32768.0))), 1966.08, 32768.0)
    return dict(inputs=inputs, out_grad=out_grad, segments=segments, windows=windows, owners=owners, weights=weights, first_moments=first_moments, second_moments=second_moments, norm_params=norm_params, norm_first=norm_first, norm_second=norm_second)


clip_level = 1.0
decay_rate = 0.1
norm_rate = 0.25
highest = lax.Precision.HIGHEST

@jax.custom_vjp
def low(v):
    return lax.optimization_barrier(v.astype(jnp.bfloat16)).astype(jnp.float32)

@jax.custom_vjp
def low_back(v):
    return v

def low_keep(v):
    return (low(v), None)

def low_pass(kept, grad):
    return (grad,)

def back_keep(v):
    return (v, None)

def back_low(kept, grad):
    return (low(grad),)
low.defvjp(low_keep, low_pass)
low_back.defvjp(back_keep, back_low)

def layer_norm(rows_in, gain, bias):
    center = rows_in - lax.optimization_barrier(jnp.mean(rows_in, axis=-1, keepdims=True))
    spread = lax.optimization_barrier(jnp.mean(center * center, axis=-1, keepdims=True))
    return center * lax.rsqrt(spread + 1e-05) * gain + bias

def slot_maps(owners):
    unit_ids = jnp.arange(UNITS, dtype=jnp.int32)
    same_owner = owners[None, :] == owners[:, None]
    earlier = unit_ids[None, :] < unit_ids[:, None]
    rank = lax.optimization_barrier(jnp.sum((same_owner & earlier).astype(jnp.int32), axis=1))
    index = (owners * SLOTS + rank).astype(jnp.int32)
    slot_ids = jnp.arange(N_SEQ * SLOTS, dtype=jnp.int32)
    match = index[None, :] == slot_ids[:, None]
    inverse = lax.optimization_barrier(jnp.sum(jnp.where(match, unit_ids[None, :], 0), axis=1)).astype(jnp.int32)
    live = jnp.any(match, axis=1)
    return (index, inverse, live)

def head_slopes():
    return jnp.power(2.0, -8.0 * (jnp.arange(HEADS, dtype=jnp.float32) + 1.0) / HEADS)

def attend(queries, keys, values, segment, windows):
    block = min(512, SEQ_LEN)
    reach = WIN // 2
    span = block + 2 * reach
    key_pad = jnp.pad(keys, ((reach, reach), (0, 0)))
    value_pad = jnp.pad(values, ((reach, reach), (0, 0)))
    segment_pad = jnp.pad(segment, (reach, reach), constant_values=-1)
    slopes = head_slopes()
    distance = jnp.abs(jnp.arange(block, dtype=jnp.int32)[:, None] + reach - jnp.arange(span, dtype=jnp.int32)[None, :])
    dist_float = distance.astype(jnp.float32)

    def one_block(number):
        start = (number * block).astype(jnp.int32)
        query_rows = lax.dynamic_slice_in_dim(queries, start, block, 0).reshape(block, HEADS, HEAD_DIM)
        key_rows = lax.dynamic_slice_in_dim(key_pad, start, span, 0).reshape(span, HEADS, HEAD_DIM)
        value_rows = lax.dynamic_slice_in_dim(value_pad, start, span, 0).reshape(span, HEADS, HEAD_DIM)
        query_seg = lax.dynamic_slice_in_dim(segment, start, block, 0)
        key_seg = lax.dynamic_slice_in_dim(segment_pad, start, span, 0)
        raw = low_back(jnp.einsum('thd,khd->htk', query_rows, key_rows, precision=highest) * 0.125)
        allowed = (query_seg[:, None] == key_seg[None, :])[None] & (2 * distance[None] < windows[:, None, None])
        logits = jnp.where(allowed, raw - slopes[:, None, None] * dist_float[None], -1e+30)
        top = lax.optimization_barrier(jnp.max(logits, axis=-1, keepdims=True))
        lifted = jnp.exp(logits - top)
        attention = lifted / lax.optimization_barrier(jnp.sum(lifted, axis=-1, keepdims=True))
        mixed = jnp.einsum('htk,khd->thd', low(attention), value_rows, precision=highest)
        peak = lax.optimization_barrier(jnp.max(jnp.where(allowed, raw, -1e+30), axis=(1, 2)))
        return (mixed.reshape(block, D), peak)
    mixed, peaks = lax.map(jax.checkpoint(one_block), jnp.arange(SEQ_LEN // block, dtype=jnp.int32))
    return (mixed.reshape(SEQ_LEN, D), lax.optimization_barrier(jnp.max(peaks, axis=0)))

def layer(tokens_in, segment, windows, w_query, w_key, w_value, w_out, w_gate_up, w_down, norms):

    def project(matrix):
        return low_back(low(jnp.dot(tokens_in, matrix, precision=highest)))
    queries = project(w_query)
    keys = project(w_key)
    values = project(w_value)
    mixed, peak = attend(queries, keys, values, segment, windows)
    mixed = low_back(low(mixed))
    branch = low_back(jnp.dot(mixed, w_out, precision=highest))
    normed_one = layer_norm(tokens_in + branch, norms[0], norms[1])
    gate_up = low_back(jnp.dot(low(normed_one), w_gate_up, precision=highest))
    hidden = low(jax.nn.gelu(gate_up[:, :FF], approximate=False) * gate_up[:, FF:])
    down = low_back(jnp.dot(hidden, w_down, precision=highest))
    result = layer_norm(normed_one + down, norms[2], norms[3])
    return (result, peak)

def join_columns(block):
    count, rows_in, cols = block.shape
    return jnp.transpose(block, (1, 0, 2)).reshape(rows_in, count * cols)

def forward(tokens_all, units, norms, segments, windows):
    groups = FF // D
    low_units = low(units)
    w_query = low_units[0]
    w_key = low_units[1]
    w_value = low_units[2]
    w_out = low_units[3]
    w_gate_up = jnp.concatenate([join_columns(low_units[4:4 + groups]), join_columns(low_units[4 + groups:4 + 2 * groups])], axis=1)
    w_down = low_units[4 + 2 * groups:].reshape(FF, D)
    checked = jax.checkpoint(layer)

    def one_sequence(operands):
        return checked(operands[0], operands[1], windows, w_query, w_key, w_value, w_out, w_gate_up, w_down, norms)
    outputs, peaks = lax.map(one_sequence, (tokens_all, segments))
    return (outputs, lax.optimization_barrier(jnp.max(peaks, axis=0)))

def adam_step(master, gradient, first, second, correction, learn_rate):
    new_first = 0.5 * first + 0.5 * gradient
    new_second = 0.5 * second + 0.5 * gradient * gradient
    normed = new_first / correction / (jnp.sqrt(new_second / correction) + 1e-08)
    return (master - learn_rate * (normed + decay_rate * master), new_first, new_second)

def reference(inputs, out_grad, segments, windows, owners, weights, first_moments, second_moments, norm_params, norm_first, norm_second):
    index, inverse, live = slot_maps(owners)
    units = weights[index]
    tokens_wide = inputs.astype(jnp.float32)

    def wrapped(tokens_all, unit_array, norms):
        return forward(tokens_all, unit_array, norms, segments, windows)
    outputs, backward, peak = jax.vjp(wrapped, tokens_wide, units, norm_params, has_aux=True)
    input_grad, unit_grads, norm_grads = backward(out_grad.astype(jnp.float32))
    correction = jnp.float32(1.0 - 0.5 ** STEP)
    unit_rate = 0.5 / D ** 0.5
    moved, unit_first, unit_second = adam_step(units, unit_grads, first_moments[index], second_moments[index], correction, unit_rate)
    factors = clip_level / jnp.maximum(peak, clip_level)
    column_scale = jnp.repeat(jnp.sqrt(factors), HEAD_DIM)
    clipped = (jnp.arange(UNITS, dtype=jnp.int32) < 2)[:, None, None]
    new_units = jnp.where(clipped, moved * column_scale[None, None, :], moved)
    new_norms, new_norm_first, new_norm_second = adam_step(norm_params, norm_grads, norm_first, norm_second, correction, norm_rate)

    def to_slots(array):
        return jnp.where(live[:, None, None], array[inverse], 0.0).astype(jnp.float32)
    new_weights = to_slots(new_units)
    return (outputs.astype(jnp.bfloat16), input_grad, to_slots(unit_grads), norm_grads, new_weights, to_slots(unit_first), to_slots(unit_second), new_weights.astype(jnp.bfloat16), new_norms, new_norm_first, new_norm_second, factors)
```

```python
import jax
import jax.numpy as jnp
from jax import lax
from jax.experimental import pallas as pl
from jax.experimental.pallas import tpu as pltpu
from jax.sharding import PartitionSpec as P

D = 768
FF = 3072
STEP = 3
clip_level = 1.0
decay_rate = 0.1
norm_rate = 0.25
LOG2E = 1.4426950408889634
NEG = -1e30
REACH = 512
QB = 256
bf16 = jnp.bfloat16
f32 = jnp.float32

def dot_nt(a, b):
    return lax.dot_general(a, b, (((1,), (1,)), ((), ())), preferred_element_type=f32)

def dot_nn(a, b):
    return lax.dot_general(a, b, (((1,), (0,)), ((), ())), preferred_element_type=f32)

def fill_bias(bias_ref, slope2):
    rows = bias_ref.shape[0]
    k = lax.broadcasted_iota(jnp.int32, (rows, QB), 0)
    q = lax.broadcasted_iota(jnp.int32, (rows, QB), 1)
    bias_ref[...] = jnp.abs(k - q - REACH).astype(f32) * (-slope2)

def fold8(x, op):
    y = x.reshape(x.shape[0] // 8, 8, x.shape[1])
    return op(y, axis=0)

def head_window(win_ref, lo_ref, hi_ref, head, qb):
    reach = (win_ref[head] - 1) >> 1
    cls = jnp.clip((reach + 127) >> 7, 2, 4)
    qpos = lax.broadcasted_iota(jnp.int32, (1, QB), 1) + (qb * QB + REACH)
    lo = jnp.maximum(lo_ref[0, :, pl.ds(qb * QB, QB)], qpos - reach)
    hi = jnp.minimum(hi_ref[0, :, pl.ds(qb * QB, QB)], qpos + reach)
    return cls, lo, hi

def fwd_kernel(win_ref, slope_ref, q_ref, k_ref, v_ref, lo_ref, hi_ref, o_ref, lse_ref, peak_ref,
               vt_ref, ot_ref, z_ref, bias_ref):
    pair = pl.program_id(0)
    seq = pl.program_id(1)
    tokens = q_ref.shape[1]
    vt_ref[...] = v_ref[0].T

    @pl.when(seq == 0)
    def _():
        peak_ref[...] = jnp.full(peak_ref.shape, NEG, f32)

    rows = lax.broadcasted_iota(jnp.int32, (QB, QB), 0)
    lane = lax.broadcasted_iota(jnp.int32, (1, 128), 1)
    for h in range(2):
        head = pair * 2 + h
        @pl.when(seq == 0)
        def _():
            fill_bias(bias_ref.at[h], slope_ref[head])
        hmask = jnp.where((lane >= h * 64) & (lane < h * 64 + 64), 0.125, 0.0)
        for qb in range(tokens // QB):
            cls, lo, hi = head_window(win_ref, lo_ref, hi_ref, head, qb)
            q = (q_ref[0, pl.ds(qb * QB, QB), :].astype(f32) * hmask).astype(bf16)

            def branch(c):
                reach = c * 128
                first = REACH - reach
                n = 1 + c
                pk = mx = None
                for t in range(n):
                    b = first + t * QB
                    s = dot_nt(k_ref[0, pl.ds(qb * QB + b, QB), :], q)
                    kk = rows + (qb * QB + b)
                    s = jnp.where((kk >= lo) & (kk <= hi), s, NEG)
                    z = s * LOG2E + bias_ref[h, pl.ds(b, QB), :]
                    a, d = fold8(s, jnp.max), fold8(z, jnp.max)
                    pk = a if t == 0 else jnp.maximum(pk, a)
                    mx = d if t == 0 else jnp.maximum(mx, d)
                    z_ref[pl.ds(t * QB, QB), :] = z
                peak_ref[h] = jnp.maximum(peak_ref[h], pk)
                m = jnp.max(mx, axis=0, keepdims=True)
                acc = total = None
                for t in range(n):
                    p = jnp.exp2(z_ref[pl.ds(t * QB, QB), :] - m)
                    e = fold8(p, jnp.sum)
                    total = e if t == 0 else total + e
                    b = first + t * QB
                    part = dot_nn(vt_ref[pl.ds(h * 64, 64), pl.ds(qb * QB + b, QB)], p.astype(bf16))
                    acc = part if t == 0 else acc + part
                total = jnp.sum(total, axis=0, keepdims=True)
                ot_ref[pl.ds(h * 64, 64), pl.ds(qb * QB, QB)] = acc * (1.0 / total)
                lse_ref[0, 0, pl.ds(h, 1), pl.ds(qb * QB, QB)] = m + jnp.log2(total)

            for c in (2, 3, 4):
                pl.when(cls == c)(lambda c=c: branch(c))
    o_ref[0] = ot_ref[...].T.astype(bf16)

def attend_fwd(windows, slopes2, q, kv, lo, hi):
    seqs, tokens, width = q.shape
    keys = kv.shape[1]
    pairs = width // 128
    smem = pl.BlockSpec(memory_space=pltpu.SMEM)
    return pl.pallas_call(
        fwd_kernel,
        grid=(pairs, seqs),
        in_specs=[
            smem, smem,
            pl.BlockSpec((1, tokens, 128), lambda p, s: (s, 0, p)),
            pl.BlockSpec((1, keys, 128), lambda p, s: (s, 0, p)),
            pl.BlockSpec((1, keys, 128), lambda p, s: (s, 0, p + pairs)),
            pl.BlockSpec((1, 1, tokens), lambda p, s: (s, 0, 0)),
            pl.BlockSpec((1, 1, tokens), lambda p, s: (s, 0, 0)),
        ],
        out_specs=[
            pl.BlockSpec((1, tokens, 128), lambda p, s: (s, 0, p)),
            pl.BlockSpec((1, 1, 2, tokens), lambda p, s: (s, p, 0, 0)),
            pl.BlockSpec((2, 8, QB), lambda p, s: (p, 0, 0)),
        ],
        out_shape=[
            jax.ShapeDtypeStruct((seqs, tokens, width), bf16),
            jax.ShapeDtypeStruct((seqs, pairs, 2, tokens), f32),
            jax.ShapeDtypeStruct((2 * pairs, 8, QB), f32),
        ],
        scratch_shapes=[
            pltpu.VMEM((128, keys), bf16),
            pltpu.VMEM((128, tokens), f32),
            pltpu.VMEM((QB + 2 * REACH, QB), f32),
            pltpu.VMEM((2, QB + 2 * REACH, QB), f32),
        ],
        compiler_params=pltpu.CompilerParams(vmem_limit_bytes=40 * 2**20),
        cost_estimate=pl.CostEstimate(flops=2 * 10**10, bytes_accessed=10**7, transcendentals=10**7),
        name="attend_fwd",
    )(windows, slopes2, q, kv, kv, lo, hi)

def bwd_kernel(win_ref, slope_ref, q_ref, k_ref, v_ref, do_ref, lo_ref, hi_ref, lse_ref, dsum_ref,
               dq_ref, dk_ref, dv_ref, kt_ref, dqt_ref, dka_ref, dva_ref, bias_ref):
    pair = pl.program_id(0)
    seq = pl.program_id(1)
    tokens = q_ref.shape[1]
    kt_ref[...] = k_ref[0].T
    dka_ref[...] = jnp.zeros(dka_ref.shape, f32)
    dva_ref[...] = jnp.zeros(dva_ref.shape, f32)
    rows = lax.broadcasted_iota(jnp.int32, (QB, QB), 0)
    lane = lax.broadcasted_iota(jnp.int32, (1, 128), 1)
    for h in range(2):
        head = pair * 2 + h
        @pl.when(seq == 0)
        def _():
            fill_bias(bias_ref.at[h], slope_ref[head])
        inside = (lane >= h * 64) & (lane < h * 64 + 64)
        qmask = jnp.where(inside, 0.125, 0.0)
        dmask = jnp.where(inside, 1.0, 0.0)
        for qb in range(tokens // QB):
            cls, lo, hi = head_window(win_ref, lo_ref, hi_ref, head, qb)
            q = (q_ref[0, pl.ds(qb * QB, QB), :].astype(f32) * qmask).astype(bf16)
            do = (do_ref[0, pl.ds(qb * QB, QB), :].astype(f32) * dmask).astype(bf16)
            lse = lse_ref[0, 0, pl.ds(h, 1), pl.ds(qb * QB, QB)]
            dsum = dsum_ref[0, 0, pl.ds(h, 1), pl.ds(qb * QB, QB)]

            def branch(c):
                first = REACH - c * 128
                dqt = None
                for t in range(1 + c):
                    b = first + t * QB
                    at = pl.ds(qb * QB + b, QB)
                    s = dot_nt(k_ref[0, at, :], q)
                    dp = dot_nt(v_ref[0, at, :], do)
                    kk = rows + (qb * QB + b)
                    z = s * LOG2E + (bias_ref[h, pl.ds(b, QB), :] - lse)
                    p = jnp.exp2(jnp.where((kk >= lo) & (kk <= hi), z, NEG))
                    ds = (p * (dp - dsum)).astype(bf16)
                    dva_ref[at, :] += dot_nn(p.astype(bf16), do)
                    dka_ref[at, :] += dot_nn(ds, q)
                    part = dot_nn(kt_ref[pl.ds(h * 64, 64), at], ds)
                    dqt = part if t == 0 else dqt + part
                dqt_ref[pl.ds(h * 64, 64), pl.ds(qb * QB, QB)] = dqt * 0.125

            for c in (2, 3, 4):
                pl.when(cls == c)(lambda c=c: branch(c))
    dq_ref[0] = dqt_ref[...].T.astype(bf16)
    dk_ref[0] = dka_ref[...].astype(bf16)
    dv_ref[0] = dva_ref[...].astype(bf16)

def attend_bwd(windows, slopes2, q, kv, do, lo, hi, lse, dsum):
    seqs, tokens, width = q.shape
    keys = kv.shape[1]
    pairs = width // 128
    smem = pl.BlockSpec(memory_space=pltpu.SMEM)
    tok = pl.BlockSpec((1, tokens, 128), lambda p, s: (s, 0, p))
    key = pl.BlockSpec((1, keys, 128), lambda p, s: (s, 0, p))
    row = pl.BlockSpec((1, 1, tokens), lambda p, s: (s, 0, 0))
    stat = pl.BlockSpec((1, 1, 2, tokens), lambda p, s: (s, p, 0, 0))
    return pl.pallas_call(
        bwd_kernel,
        grid=(pairs, seqs),
        in_specs=[smem, smem, tok, key, pl.BlockSpec((1, keys, 128), lambda p, s: (s, 0, p + pairs)), tok, row, row, stat, stat],
        out_specs=[tok, key, key],
        out_shape=[
            jax.ShapeDtypeStruct((seqs, tokens, width), bf16),
            jax.ShapeDtypeStruct((seqs, keys, width), bf16),
            jax.ShapeDtypeStruct((seqs, keys, width), bf16),
        ],
        scratch_shapes=[
            pltpu.VMEM((128, keys), bf16),
            pltpu.VMEM((128, tokens), f32),
            pltpu.VMEM((keys, 128), f32),
            pltpu.VMEM((keys, 128), f32),
            pltpu.VMEM((2, QB + 2 * REACH, QB), f32),
        ],
        compiler_params=pltpu.CompilerParams(vmem_limit_bytes=40 * 2**20),
        cost_estimate=pl.CostEstimate(flops=5 * 10**10, bytes_accessed=2 * 10**7, transcendentals=10**7),
        name="attend_bwd",
    )(windows, slopes2, q, kv, kv, do, lo, hi, lse, dsum)

def shifted(value, axis, by):
    peers = lax.axis_size(axis)
    pairs = [(i, i + by) for i in range(peers) if 0 <= i + by < peers]
    return lax.ppermute(value, axis, pairs)


def swapped(value, axis, bit):
    peers = lax.axis_size(axis)
    return lax.ppermute(value, axis, [(i, i ^ bit) for i in range(peers)])


def layer_norm(rows_in):
    center = rows_in - jnp.mean(rows_in, axis=-1, keepdims=True)
    spread = jnp.mean(center * center, axis=-1, keepdims=True)
    scale = lax.rsqrt(spread + 1e-05)
    return center * scale, scale


def layer_norm_back(grad, hat, scale, gain):
    inner = grad * gain
    mean_one = jnp.mean(inner, axis=-1, keepdims=True)
    mean_two = jnp.mean(inner * hat, axis=-1, keepdims=True)
    back = scale * (inner - mean_one - hat * mean_two)
    return back, jnp.sum(grad * hat, axis=0), jnp.sum(grad, axis=0)


def pick_units(slot_of, sources, count):
    slots, rows, width = sources[0].shape

    def kernel(slot_ref, *refs):
        out_ref = refs[-1]
        for u in range(count):
            at = pl.ds(u * width, width)
            for number, ref in enumerate(refs[:-1]):

                @pl.when(slot_ref[0, u] == number)
                def _(ref=ref, u=u, at=at):
                    out_ref[:, at] = ref[slot_ref[1, u]]

    vmem = pl.BlockSpec(memory_space=pltpu.VMEM)
    return pl.pallas_call(
        kernel,
        in_specs=[pl.BlockSpec(memory_space=pltpu.SMEM)] + [vmem] * len(sources),
        out_specs=vmem,
        out_shape=jax.ShapeDtypeStruct((rows, count * width), sources[0].dtype),
        compiler_params=pltpu.CompilerParams(vmem_limit_bytes=24 * 2**20),
        name="pick_units",
    )(slot_of, *sources)


def to_slots(unit_of, columns, slots, width):
    rows = columns.shape[0]

    def kernel(unit_ref, col_ref, out_ref):
        for s in range(slots):
            unit = unit_ref[s]

            @pl.when(unit >= 0)
            def _(s=s, unit=unit):
                out_ref[s] = col_ref[:, pl.ds(pl.multiple_of(unit * width, 128), width)]

            @pl.when(unit < 0)
            def _(s=s):
                out_ref[s] = jnp.zeros((rows, width), out_ref.dtype)

    vmem = pl.BlockSpec(memory_space=pltpu.VMEM)
    return pl.pallas_call(
        kernel,
        in_specs=[pl.BlockSpec(memory_space=pltpu.SMEM), vmem],
        out_specs=vmem,
        out_shape=jax.ShapeDtypeStruct((slots, rows, width), columns.dtype),
        compiler_params=pltpu.CompilerParams(vmem_limit_bytes=24 * 2**20),
        name="to_slots",
    )(unit_of, columns)


def adam_slots(unit_of, weights, first, second, grads, scale, correction, rate):
    slots, rows, width = weights.shape

    def kernel(unit_ref, w_ref, m_ref, v_ref, scale_ref, *refs):
        grad_refs, (g_out, w_out, m_out, v_out, low_out) = refs[:-5], refs[-5:]
        unit = unit_ref[pl.program_id(0)]
        live = unit >= 0
        g = grad_refs[0][0].astype(f32)
        for ref in grad_refs[1:]:
            g = g + ref[0].astype(f32)
        g = jnp.where(live, g, 0.0)
        w = w_ref[0]
        m = 0.5 * m_ref[0] + 0.5 * g
        v = 0.5 * v_ref[0] + 0.5 * g * g
        step = m * (1.0 / correction) / (jnp.sqrt(v * (1.0 / correction)) + 1e-08)
        moved = w - rate * (step + decay_rate * w)
        moved = jnp.where((unit == 0) | (unit == 1), moved * scale_ref[...], moved)
        moved = jnp.where(live, moved, 0.0)
        g_out[0] = g
        w_out[0] = moved
        m_out[0] = jnp.where(live, m, 0.0)
        v_out[0] = jnp.where(live, v, 0.0)
        low_out[0] = moved.astype(bf16)

    block = pl.BlockSpec((1, rows, width), lambda s: (s, 0, 0))
    wide = jax.ShapeDtypeStruct(weights.shape, f32)
    return pl.pallas_call(
        kernel,
        grid=(slots,),
        in_specs=[pl.BlockSpec(memory_space=pltpu.SMEM), block, block, block,
                  pl.BlockSpec((1, width), lambda s: (0, 0))] + [block] * len(grads),
        out_specs=[block] * 5,
        out_shape=[wide] * 4 + [jax.ShapeDtypeStruct(weights.shape, bf16)],
        compiler_params=pltpu.CompilerParams(vmem_limit_bytes=24 * 2**20),
        name="adam_slots",
    )(unit_of, weights, first, second, scale, *grads)


def adam_step(master, gradient, first, second, correction, learn_rate):
    new_first = 0.5 * first + 0.5 * gradient
    new_second = 0.5 * second + 0.5 * gradient * gradient
    normed = new_first / correction / (jnp.sqrt(new_second / correction) + 1e-08)
    return (master - learn_rate * (normed + decay_rate * master), new_first, new_second)


def dot_tn(a, b):
    return lax.dot_general(a, b, (((0,), (0,)), ((), ())), preferred_element_type=f32)


def gelu_parts(gate):
    cdf = 0.5 * (1.0 + lax.erf(gate * 0.7071067811865476))
    density = 0.3989422804014327 * jnp.exp(-0.5 * gate * gate)
    return cdf, density


def on_device(inputs, out_grad, segments, windows, owners, weights, first_moments, second_moments,
              norm_params, norm_first, norm_second):
    seqs, tokens, width = inputs.shape
    rows = seqs * tokens
    heads = windows.shape[0]
    slots = weights.shape[0]
    owner_count = lax.axis_size("seq")
    me = lax.axis_index("seq")
    seq_len = segments.shape[1]
    keys = tokens + 2 * REACH
    pieces = REACH // tokens
    groups = FF // width
    units = owners.shape[0]
    rest = units - 3

    ids = jnp.arange(units, dtype=jnp.int32)
    before = (owners[None, :] == owners[:, None]) & (ids[None, :] < ids[:, None])
    rank = jnp.sum(before.astype(jnp.int32), axis=1)
    slot_ids = jnp.arange(owner_count * slots, dtype=jnp.int32)
    match = (owners * slots + rank)[None, :] == slot_ids[:, None]
    unit_of = jnp.max(jnp.where(match, ids[None, :], -1), axis=1)
    my_units = lax.dynamic_slice_in_dim(unit_of, me * slots, slots, 0)

    low = weights.astype(bf16)
    if owner_count == 2:
        place = jnp.stack([jnp.where(owners == me, 0, 1), rank])
        own_first = pick_units(place[:, :3] * jnp.array([[0], [1]], jnp.int32), [low], 3)
        got_first = swapped(own_first, "seq", 1)
        mine = jnp.repeat(owners[:3] == me, width)[None, :]
        picked_first = jnp.where(mine, own_first, got_first)
        sources = [low, swapped(low, "seq", 1)]
    else:
        every = lax.all_gather(low, "seq", axis=0, tiled=True)
        place = jnp.stack([jnp.zeros_like(owners), owners * slots + rank])
        sources = [every]
        picked_first = pick_units(place[:, :3], sources, 3)
    w_first = lax.all_gather(picked_first, "ctx", axis=0, tiled=True)
    picked_rest = pick_units(place[:, 3:], sources, rest)
    picked_rest, w_first = lax.optimization_barrier((picked_rest, w_first))
    w_rest = lax.all_gather(picked_rest, "ctx", axis=0, tiled=True)

    left = [shifted(inputs, "ctx", pieces - n) for n in range(pieces)]
    right = [shifted(inputs, "ctx", -(n + 1)) for n in range(pieces)]
    x_ext = jnp.concatenate(left + [inputs] + right, axis=1)

    start = lax.axis_index("ctx") * tokens
    padded = jnp.pad(segments, ((0, 0), (REACH, 0)), constant_values=-1)
    padded = jnp.pad(padded, ((0, 0), (0, REACH)), constant_values=1 << 20)
    key_seg = lax.dynamic_slice_in_dim(padded, start, keys, 1)
    query_seg = key_seg[:, REACH : REACH + tokens]
    lo = jnp.sum((key_seg[:, :, None] < query_seg[:, None, :]).astype(jnp.int32), axis=1)[:, None]
    hi = jnp.sum((key_seg[:, :, None] <= query_seg[:, None, :]).astype(jnp.int32), axis=1)[:, None] - 1
    slopes2 = jnp.power(2.0, -8.0 * (jnp.arange(heads, dtype=f32) + 1.0) / heads) * LOG2E

    w_q, w_kv = w_first[:, :width], w_first[:, width:]
    x = inputs.reshape(rows, width)
    q = dot_nn(x, w_q).astype(bf16).reshape(seqs, tokens, width)
    kv = dot_nn(x_ext.reshape(seqs * keys, width), w_kv).astype(bf16).reshape(seqs, keys, 2 * width)
    mixed, lse, peaks = attend_fwd(windows, slopes2, q, kv, lo, hi)
    peak = jnp.max(peaks, axis=(1, 2))
    o = mixed.reshape(rows, width)

    w_out = w_rest[:, :width]
    w_gate = w_rest[:, width : width + FF]
    w_up = w_rest[:, width + FF : width + 2 * FF]
    w_down = jnp.concatenate(
        [w_rest[:, width + 2 * FF + g * width : width + 2 * FF + (g + 1) * width] for g in range(groups)], axis=0
    )
    first_sum = x.astype(f32) + dot_nn(o, w_out)
    hat_one, scale_one = layer_norm(first_sum)
    y1 = hat_one * norm_params[0] + norm_params[1]
    y_low = y1.astype(bf16)
    gate = dot_nn(y_low, w_gate)
    up = dot_nn(y_low, w_up)
    cdf, density = gelu_parts(gate)
    hidden = (gate * cdf * up).astype(bf16)
    second_sum = y1 + dot_nn(hidden, w_down)
    hat_two, scale_two = layer_norm(second_sum)
    output = (hat_two * norm_params[2] + norm_params[3]).astype(bf16).reshape(seqs, tokens, width)

    out_wide = out_grad.reshape(rows, width).astype(f32)
    second_grad, gain_two, bias_two = layer_norm_back(out_wide, hat_two, scale_two, norm_params[2])
    f_grad = second_grad.astype(bf16)
    hidden_grad = dot_nt(f_grad, w_down)
    gate_grad = (hidden_grad * up * (cdf + gate * density)).astype(bf16)
    up_grad = (hidden_grad * (gate * cdf)).astype(bf16)
    y1_grad = second_grad + dot_nt(gate_grad, w_gate) + dot_nt(up_grad, w_up)
    first_grad, gain_one, bias_one = layer_norm_back(y1_grad, hat_one, scale_one, norm_params[0])
    a_grad = first_grad.astype(bf16)
    rest_grads = jnp.concatenate(
        [dot_tn(o, a_grad).astype(bf16), dot_tn(y_low, gate_grad).astype(bf16), dot_tn(y_low, up_grad).astype(bf16)]
        + [dot_tn(hidden[:, g * width : (g + 1) * width], f_grad).astype(bf16) for g in range(groups)],
        axis=1,
    )
    rest_sums = lax.psum_scatter(rest_grads, "ctx", scatter_dimension=0, tiled=True)

    o_grad = dot_nt(a_grad, w_out).astype(bf16)
    dsum = jnp.sum((o.astype(f32) * o_grad.astype(f32)).reshape(seqs, tokens, heads // 2, 2, width // heads), axis=-1)
    dsum = jnp.transpose(dsum, (0, 2, 3, 1))
    dq, dk, dv = attend_bwd(windows, slopes2, q, kv, o_grad.reshape(seqs, tokens, width), lo, hi, lse, dsum)

    xe = x_ext.reshape(seqs * keys, width)
    dk_flat, dv_flat = dk.reshape(seqs * keys, width), dv.reshape(seqs * keys, width)
    first_grads = jnp.concatenate(
        [dot_tn(x, dq.reshape(rows, width)).astype(bf16), dot_tn(xe, dk_flat).astype(bf16), dot_tn(xe, dv_flat).astype(bf16)],
        axis=1,
    )
    first_sums = lax.psum_scatter(first_grads, "ctx", scatter_dimension=0, tiled=True)

    key_part = (dot_nt(dk_flat, w_kv[:, :width]) + dot_nt(dv_flat, w_kv[:, width:])).reshape(seqs, keys, width)
    input_grad = first_grad.reshape(seqs, tokens, width) + dot_nt(dq.reshape(rows, width), w_q).reshape(seqs, tokens, width)
    input_grad = input_grad + key_part[:, REACH : REACH + tokens]
    for n in range(pieces):
        to_left = key_part[:, n * tokens : (n + 1) * tokens].astype(bf16)
        to_right = key_part[:, REACH + (n + 1) * tokens : REACH + (n + 2) * tokens].astype(bf16)
        input_grad = input_grad + shifted(to_left, "ctx", n - pieces).astype(f32)
        input_grad = input_grad + shifted(to_right, "ctx", n + 1).astype(f32)

    small = jnp.concatenate(
        [jnp.stack([gain_one, bias_one, gain_two, bias_two]), jnp.pad(peak, (0, width - heads))[None], jnp.zeros((3, width), f32)]
    )
    is_peak = (jnp.arange(8) == 4)[:, None]
    for axis in ("ctx", "seq"):
        bit = 1
        while bit < lax.axis_size(axis):
            other = swapped(small, axis, bit)
            small = jnp.where(is_peak, jnp.maximum(small, other), small + other)
            bit *= 2
    norm_grads = small[:4]
    factors = clip_level / jnp.maximum(small[4, :heads], clip_level)
    column_scale = jnp.repeat(jnp.sqrt(factors), width // heads)[None, :]
    correction = 1.0 - 0.5**STEP

    def owned(columns, lowest):
        count = columns.shape[1] // width
        local = unit_of - lowest
        local = jnp.where((local >= 0) & (local < count), local, -1)
        if owner_count == 2:
            keep = to_slots(lax.dynamic_slice_in_dim(local, me * slots, slots, 0), columns, slots, width)
            give = to_slots(lax.dynamic_slice_in_dim(local, (1 - me) * slots, slots, 0), columns, slots, width)
            return [keep, swapped(give, "seq", 1)]
        every = to_slots(local, columns, owner_count * slots, width)
        return [lax.psum_scatter(every, "seq", scatter_dimension=0, tiled=True)]

    parts = owned(rest_sums, 3) + owned(first_sums, 0)
    weight_grads, new_weights, new_first, new_second, weights_low = adam_slots(
        my_units, weights, first_moments, second_moments, parts, column_scale, correction, 0.5 / D**0.5
    )
    new_norms, new_norm_first, new_norm_second = adam_step(
        norm_params, norm_grads, norm_first, norm_second, correction, norm_rate
    )
    return (output, input_grad, weight_grads, norm_grads, new_weights, new_first, new_second, weights_low,
            new_norms, new_norm_first, new_norm_second, factors)


def solution(mesh):
    block = P("seq", "ctx", None)
    return jax.shard_map(
        on_device,
        mesh=mesh,
        in_specs=(block, block, P("seq", None), P(), P(), block, block, block, P(), P(), P()),
        out_specs=(block, block, block, P(), block, block, block, block, P(), P(), P(), P()),
        check_vma=False,
    )
```

```python
import jax
import jax.numpy as jnp
from jax import lax
from jax.experimental import pallas as pl
from jax.experimental.pallas import tpu as pltpu
from jax.sharding import PartitionSpec as P

D = 768
FF = 3072
STEP = 3
clip_level = 1.0
decay_rate = 0.1
norm_rate = 0.25
LOG2E = 1.4426950408889634
NEG = -1e30
REACH = 512
QB = 256
bf16 = jnp.bfloat16
f32 = jnp.float32

def dot_nt(a, b):
    return lax.dot_general(a, b, (((1,), (1,)), ((), ())), preferred_element_type=f32)

def dot_nn(a, b):
    return lax.dot_general(a, b, (((1,), (0,)), ((), ())), preferred_element_type=f32)

def fill_bias(bias_ref, slope2):
    rows = bias_ref.shape[0]
    k = lax.broadcasted_iota(jnp.int32, (rows, QB), 0)
    q = lax.broadcasted_iota(jnp.int32, (rows, QB), 1)
    bias_ref[...] = jnp.abs(k - q - REACH).astype(f32) * (-slope2)

def fold8(x, op):
    y = x.reshape(x.shape[0] // 8, 8, x.shape[1])
    return op(y, axis=0)

def head_window(win_ref, lo_ref, hi_ref, head, qb):
    reach = (win_ref[head] - 1) >> 1
    cls = jnp.clip((reach + 127) >> 7, 2, 4)
    qpos = lax.broadcasted_iota(jnp.int32, (1, QB), 1) + (qb * QB + REACH)
    lo = jnp.maximum(lo_ref[0, :, pl.ds(qb * QB, QB)], qpos - reach)
    hi = jnp.minimum(hi_ref[0, :, pl.ds(qb * QB, QB)], qpos + reach)
    return cls, lo, hi

def fwd_kernel(win_ref, slope_ref, q_ref, k_ref, v_ref, lo_ref, hi_ref, o_ref, lse_ref, peak_ref,
               vt_ref, ot_ref, z_ref, bias_ref):
    pair = pl.program_id(0)
    seq = pl.program_id(1)
    tokens = q_ref.shape[1]
    vt_ref[...] = v_ref[0].T

    @pl.when(seq == 0)
    def _():
        peak_ref[...] = jnp.full(peak_ref.shape, NEG, f32)

    rows = lax.broadcasted_iota(jnp.int32, (QB, QB), 0)
    lane = lax.broadcasted_iota(jnp.int32, (1, 128), 1)
    for h in range(2):
        head = pair * 2 + h
        @pl.when(seq == 0)
        def _():
            fill_bias(bias_ref.at[h], slope_ref[head])
        hmask = jnp.where((lane >= h * 64) & (lane < h * 64 + 64), 0.125, 0.0)
        for qb in range(tokens // QB):
            cls, lo, hi = head_window(win_ref, lo_ref, hi_ref, head, qb)
            q = (q_ref[0, pl.ds(qb * QB, QB), :].astype(f32) * hmask).astype(bf16)

            def branch(c):
                reach = c * 128
                first = REACH - reach
                n = 1 + c
                pk = mx = None
                for t in range(n):
                    b = first + t * QB
                    s = dot_nt(k_ref[0, pl.ds(qb * QB + b, QB), :], q)
                    kk = rows + (qb * QB + b)
                    s = jnp.where((kk >= lo) & (kk <= hi), s, NEG)
                    z = s * LOG2E + bias_ref[h, pl.ds(b, QB), :]
                    a, d = fold8(s, jnp.max), fold8(z, jnp.max)
                    pk = a if t == 0 else jnp.maximum(pk, a)
                    mx = d if t == 0 else jnp.maximum(mx, d)
                    z_ref[pl.ds(t * QB, QB), :] = z
                peak_ref[h] = jnp.maximum(peak_ref[h], pk)
                m = jnp.max(mx, axis=0, keepdims=True)
                acc = total = None
                for t in range(n):
                    p = jnp.exp2(z_ref[pl.ds(t * QB, QB), :] - m)
                    e = fold8(p, jnp.sum)
                    total = e if t == 0 else total + e
                    b = first + t * QB
                    part = dot_nn(vt_ref[pl.ds(h * 64, 64), pl.ds(qb * QB + b, QB)], p.astype(bf16))
                    acc = part if t == 0 else acc + part
                total = jnp.sum(total, axis=0, keepdims=True)
                ot_ref[pl.ds(h * 64, 64), pl.ds(qb * QB, QB)] = acc * (1.0 / total)
                lse_ref[0, 0, pl.ds(h, 1), pl.ds(qb * QB, QB)] = m + jnp.log2(total)

            for c in (2, 3, 4):
                pl.when(cls == c)(lambda c=c: branch(c))
    o_ref[0] = ot_ref[...].T.astype(bf16)

def attend_fwd(windows, slopes2, q, kv, lo, hi):
    seqs, tokens, width = q.shape
    keys = kv.shape[1]
    pairs = width // 128
    smem = pl.BlockSpec(memory_space=pltpu.SMEM)
    return pl.pallas_call(
        fwd_kernel,
        grid=(pairs, seqs),
        in_specs=[
            smem, smem,
            pl.BlockSpec((1, tokens, 128), lambda p, s: (s, 0, p)),
            pl.BlockSpec((1, keys, 128), lambda p, s: (s, 0, p)),
            pl.BlockSpec((1, keys, 128), lambda p, s: (s, 0, p + pairs)),
            pl.BlockSpec((1, 1, tokens), lambda p, s: (s, 0, 0)),
            pl.BlockSpec((1, 1, tokens), lambda p, s: (s, 0, 0)),
        ],
        out_specs=[
            pl.BlockSpec((1, tokens, 128), lambda p, s: (s, 0, p)),
            pl.BlockSpec((1, 1, 2, tokens), lambda p, s: (s, p, 0, 0)),
            pl.BlockSpec((2, 8, QB), lambda p, s: (p, 0, 0)),
        ],
        out_shape=[
            jax.ShapeDtypeStruct((seqs, tokens, width), bf16),
            jax.ShapeDtypeStruct((seqs, pairs, 2, tokens), f32),
            jax.ShapeDtypeStruct((2 * pairs, 8, QB), f32),
        ],
        scratch_shapes=[
            pltpu.VMEM((128, keys), bf16),
            pltpu.VMEM((128, tokens), f32),
            pltpu.VMEM((QB + 2 * REACH, QB), f32),
            pltpu.VMEM((2, QB + 2 * REACH, QB), f32),
        ],
        compiler_params=pltpu.CompilerParams(vmem_limit_bytes=40 * 2**20),
        cost_estimate=pl.CostEstimate(flops=2 * 10**10, bytes_accessed=10**7, transcendentals=10**7),
        name="attend_fwd",
    )(windows, slopes2, q, kv, kv, lo, hi)

def bwd_kernel(win_ref, slope_ref, q_ref, k_ref, v_ref, do_ref, o_ref, lo_ref, hi_ref, lse_ref,
               dq_ref, dk_ref, dv_ref, kt_ref, dqt_ref, dka_ref, dva_ref, bias_ref):
    pair = pl.program_id(0)
    seq = pl.program_id(1)
    tokens = q_ref.shape[1]
    kt_ref[...] = k_ref[0].T
    dka_ref[...] = jnp.zeros(dka_ref.shape, f32)
    dva_ref[...] = jnp.zeros(dva_ref.shape, f32)
    rows = lax.broadcasted_iota(jnp.int32, (QB, QB), 0)
    lane = lax.broadcasted_iota(jnp.int32, (1, 128), 1)
    ones = jnp.ones((16, 128), bf16)
    for h in range(2):
        head = pair * 2 + h
        @pl.when(seq == 0)
        def _():
            fill_bias(bias_ref.at[h], slope_ref[head])
        inside = (lane >= h * 64) & (lane < h * 64 + 64)
        qmask = jnp.where(inside, 0.125, 0.0)
        dmask = jnp.where(inside, 1.0, 0.0)
        for qb in range(tokens // QB):
            cls, lo, hi = head_window(win_ref, lo_ref, hi_ref, head, qb)
            q = (q_ref[0, pl.ds(qb * QB, QB), :].astype(f32) * qmask).astype(bf16)
            do = (do_ref[0, pl.ds(qb * QB, QB), :].astype(f32) * dmask).astype(bf16)
            lse = lse_ref[0, 0, pl.ds(h, 1), pl.ds(qb * QB, QB)]
            prod = do.astype(f32) * o_ref[0, pl.ds(qb * QB, QB), :].astype(f32)
            prod_hi = prod.astype(bf16)
            prod_lo = (prod - prod_hi.astype(f32)).astype(bf16)
            dsum = (dot_nt(ones, prod_hi) + dot_nt(ones, prod_lo))[:1]

            def branch(c):
                first = REACH - c * 128
                dqt = None
                for t in range(1 + c):
                    b = first + t * QB
                    at = pl.ds(qb * QB + b, QB)
                    s = dot_nt(k_ref[0, at, :], q)
                    dp = dot_nt(v_ref[0, at, :], do)
                    kk = rows + (qb * QB + b)
                    z = s * LOG2E + (bias_ref[h, pl.ds(b, QB), :] - lse)
                    p = jnp.exp2(jnp.where((kk >= lo) & (kk <= hi), z, NEG))
                    ds = (p * (dp - dsum)).astype(bf16)
                    dva_ref[at, :] += dot_nn(p.astype(bf16), do)
                    dka_ref[at, :] += dot_nn(ds, q)
                    part = dot_nn(kt_ref[pl.ds(h * 64, 64), at], ds)
                    dqt = part if t == 0 else dqt + part
                dqt_ref[pl.ds(h * 64, 64), pl.ds(qb * QB, QB)] = dqt * 0.125

            for c in (2, 3, 4):
                pl.when(cls == c)(lambda c=c: branch(c))
    dq_ref[0] = dqt_ref[...].T.astype(bf16)
    dk_ref[0] = dka_ref[...].astype(bf16)
    dv_ref[0] = dva_ref[...].astype(bf16)

def attend_bwd(windows, slopes2, q, kv, do, o, lo, hi, lse):
    seqs, tokens, width = q.shape
    keys = kv.shape[1]
    pairs = width // 128
    smem = pl.BlockSpec(memory_space=pltpu.SMEM)
    tok = pl.BlockSpec((1, tokens, 128), lambda p, s: (s, 0, p))
    key = pl.BlockSpec((1, keys, 128), lambda p, s: (s, 0, p))
    row = pl.BlockSpec((1, 1, tokens), lambda p, s: (s, 0, 0))
    stat = pl.BlockSpec((1, 1, 2, tokens), lambda p, s: (s, p, 0, 0))
    return pl.pallas_call(
        bwd_kernel,
        grid=(pairs, seqs),
        in_specs=[smem, smem, tok, key, pl.BlockSpec((1, keys, 128), lambda p, s: (s, 0, p + pairs)), tok, tok, row, row, stat],
        out_specs=[tok, key, key],
        out_shape=[
            jax.ShapeDtypeStruct((seqs, tokens, width), bf16),
            jax.ShapeDtypeStruct((seqs, keys, width), bf16),
            jax.ShapeDtypeStruct((seqs, keys, width), bf16),
        ],
        scratch_shapes=[
            pltpu.VMEM((128, keys), bf16),
            pltpu.VMEM((128, tokens), f32),
            pltpu.VMEM((keys, 128), f32),
            pltpu.VMEM((keys, 128), f32),
            pltpu.VMEM((2, QB + 2 * REACH, QB), f32),
        ],
        compiler_params=pltpu.CompilerParams(vmem_limit_bytes=40 * 2**20),
        cost_estimate=pl.CostEstimate(flops=5 * 10**10, bytes_accessed=2 * 10**7, transcendentals=10**7),
        name="attend_bwd",
    )(windows, slopes2, q, kv, kv, do, o, lo, hi, lse)

def shifted(value, axis, by):
    peers = lax.axis_size(axis)
    pairs = [(i, i + by) for i in range(peers) if 0 <= i + by < peers]
    return lax.ppermute(value, axis, pairs)


def swapped(value, axis, bit):
    peers = lax.axis_size(axis)
    return lax.ppermute(value, axis, [(i, i ^ bit) for i in range(peers)])


def layer_norm(rows_in):
    center = rows_in - jnp.mean(rows_in, axis=-1, keepdims=True)
    spread = jnp.mean(center * center, axis=-1, keepdims=True)
    scale = lax.rsqrt(spread + 1e-05)
    return center * scale, scale


def layer_norm_back(grad, hat, scale, gain):
    inner = grad * gain
    mean_one = jnp.mean(inner, axis=-1, keepdims=True)
    mean_two = jnp.mean(inner * hat, axis=-1, keepdims=True)
    back = scale * (inner - mean_one - hat * mean_two)
    return back, jnp.sum(grad * hat, axis=0, keepdims=True), jnp.sum(grad, axis=0, keepdims=True)


def exchange_scatter(value, axis):
    peers = lax.axis_size(axis)
    me = lax.axis_index(axis)
    rows = value.shape[0] // peers
    bit = 1
    value = value.reshape((peers, rows) + value.shape[1:])
    while bit < peers:
        count = value.shape[0]
        split = value.reshape((count // 2, 2) + value.shape[1:])
        side = (me // bit) % 2
        keep = lax.dynamic_index_in_dim(split, side, 1, False)
        give = lax.dynamic_index_in_dim(split, 1 - side, 1, False)
        got = swapped(give, axis, bit)
        value = (keep.astype(f32) + got.astype(f32)).astype(value.dtype)
        bit *= 2
    return value[0]


def pick_units(slot_of, sources, count):
    slots, rows, width = sources[0].shape

    def kernel(slot_ref, *refs):
        out_ref = refs[-1]
        for u in range(count):
            at = pl.ds(u * width, width)
            for number, ref in enumerate(refs[:-1]):

                @pl.when(slot_ref[0, u] == number)
                def _(ref=ref, u=u, at=at):
                    out_ref[:, at] = ref[slot_ref[1, u]]

    vmem = pl.BlockSpec(memory_space=pltpu.VMEM)
    return pl.pallas_call(
        kernel,
        in_specs=[pl.BlockSpec(memory_space=pltpu.SMEM)] + [vmem] * len(sources),
        out_specs=vmem,
        out_shape=jax.ShapeDtypeStruct((rows, count * width), sources[0].dtype),
        compiler_params=pltpu.CompilerParams(vmem_limit_bytes=24 * 2**20),
        name="pick_units",
    )(slot_of, *sources)


def to_slots(unit_of, columns, slots, width):
    rows = columns.shape[0]

    def kernel(unit_ref, col_ref, out_ref):
        for s in range(slots):
            unit = unit_ref[s]

            @pl.when(unit >= 0)
            def _(s=s, unit=unit):
                out_ref[s] = col_ref[:, pl.ds(pl.multiple_of(unit * width, 128), width)]

            @pl.when(unit < 0)
            def _(s=s):
                out_ref[s] = jnp.zeros((rows, width), out_ref.dtype)

    vmem = pl.BlockSpec(memory_space=pltpu.VMEM)
    return pl.pallas_call(
        kernel,
        in_specs=[pl.BlockSpec(memory_space=pltpu.SMEM), vmem],
        out_specs=vmem,
        out_shape=jax.ShapeDtypeStruct((slots, rows, width), columns.dtype),
        compiler_params=pltpu.CompilerParams(vmem_limit_bytes=24 * 2**20),
        name="to_slots",
    )(unit_of, columns)


def adam_slots(unit_of, weights, first, second, grads, scale, correction, rate):
    slots, rows, width = weights.shape

    def kernel(unit_ref, w_ref, m_ref, v_ref, scale_ref, *refs):
        grad_refs, (g_out, w_out, m_out, v_out, low_out) = refs[:-5], refs[-5:]
        unit = unit_ref[pl.program_id(0)]
        live = unit >= 0
        g = grad_refs[0][0].astype(f32)
        for ref in grad_refs[1:]:
            g = g + ref[0].astype(f32)
        g = jnp.where(live, g, 0.0)
        w = w_ref[0]
        m = 0.5 * m_ref[0] + 0.5 * g
        v = 0.5 * v_ref[0] + 0.5 * g * g
        step = m * (1.0 / correction) / (jnp.sqrt(v * (1.0 / correction)) + 1e-08)
        moved = w - rate * (step + decay_rate * w)
        moved = jnp.where((unit == 0) | (unit == 1), moved * scale_ref[...], moved)
        moved = jnp.where(live, moved, 0.0)
        g_out[0] = g
        w_out[0] = moved
        m_out[0] = jnp.where(live, m, 0.0)
        v_out[0] = jnp.where(live, v, 0.0)
        low_out[0] = moved.astype(bf16)

    block = pl.BlockSpec((1, rows, width), lambda s: (s, 0, 0))
    wide = jax.ShapeDtypeStruct(weights.shape, f32)
    return pl.pallas_call(
        kernel,
        grid=(slots,),
        in_specs=[pl.BlockSpec(memory_space=pltpu.SMEM), block, block, block,
                  pl.BlockSpec((1, width), lambda s: (0, 0))] + [block] * len(grads),
        out_specs=[block] * 5,
        out_shape=[wide] * 4 + [jax.ShapeDtypeStruct(weights.shape, bf16)],
        compiler_params=pltpu.CompilerParams(vmem_limit_bytes=24 * 2**20),
        name="adam_slots",
    )(unit_of, weights, first, second, scale, *grads)


def adam_step(master, gradient, first, second, correction, learn_rate):
    new_first = 0.5 * first + 0.5 * gradient
    new_second = 0.5 * second + 0.5 * gradient * gradient
    normed = new_first / correction / (jnp.sqrt(new_second / correction) + 1e-08)
    return (master - learn_rate * (normed + decay_rate * master), new_first, new_second)


def dot_tn(a, b):
    return lax.dot_general(a, b, (((0,), (0,)), ((), ())), preferred_element_type=f32)


def gelu_parts(gate):
    cdf = 0.5 * (1.0 + lax.erf(gate * 0.7071067811865476))
    density = 0.3989422804014327 * jnp.exp(-0.5 * gate * gate)
    return cdf, density


RB = 256
CHUNK = 256


def ffn_kernel(o_ref, x_ref, og_ref, wo_ref, wg_ref, wu_ref, wd_ref, norm_ref,
               out_ref, first_ref, ograd_ref, small_ref, grads_ref,
               hat_ref, scale_ref, acc_ref, a_ref, b_ref, h_ref, ylow_ref, ylowt_ref, fgrad_ref,
               gg_ref, ug_ref, stage_g, stage_u, stage_d, stage_o, sems):
    step = pl.program_id(0)
    rows, width = x_ref.shape
    chunk = wg_ref.shape[1]
    chunks = FF // chunk
    blocks = rows // RB

    def at(i):
        return pl.ds(i * RB, RB)

    def copies(j):
        slot = lax.rem(j, 2)
        column = pl.multiple_of(width + j * chunk, 128)
        per = width // chunk
        return (
            pltpu.make_async_copy(stage_g.at[slot], grads_ref.at[:, pl.ds(column, chunk)], sems.at[slot, 0]),
            pltpu.make_async_copy(stage_u.at[slot], grads_ref.at[:, pl.ds(column + FF, chunk)], sems.at[slot, 1]),
            pltpu.make_async_copy(
                stage_d.at[slot],
                grads_ref.at[pl.ds(pl.multiple_of(lax.rem(j, per) * chunk, 128), chunk),
                             pl.ds(pl.multiple_of(width + 2 * FF + lax.div(j, per) * width, 128), width)],
                sems.at[slot, 2],
            ),
        )

    @pl.when(step == 0)
    def _():
        for i in range(blocks):
            total = x_ref[at(i), :].astype(f32) + dot_nn(o_ref[at(i), :], wo_ref[...])
            hat, scale = layer_norm(total)
            y1 = hat * norm_ref[0:1, :] + norm_ref[1:2, :]
            hat_ref[at(i), :] = hat
            scale_ref[at(i), :] = scale
            acc_ref[at(i), :] = y1
            ylow_ref[at(i), :] = y1.astype(bf16)
            ylowt_ref[:, at(i)] = y1.T.astype(bf16)

    @pl.when(step < chunks)
    def _():
        for i in range(blocks):
            y = ylow_ref[at(i), :]
            gate = dot_nn(y, wg_ref[...])
            up = dot_nn(y, wu_ref[...])
            cdf, density = gelu_parts(gate)
            a = gate * cdf
            hidden = (a * up).astype(bf16)
            a_ref[step, at(i), :] = a.astype(bf16)
            b_ref[step, at(i), :] = (up * (cdf + gate * density)).astype(bf16)
            h_ref[step, at(i), :] = hidden
            acc_ref[at(i), :] += dot_nn(hidden, wd_ref[...])

    @pl.when(step == chunks)
    def _():
        gain = bias = None
        for i in range(blocks):
            hat, scale = layer_norm(acc_ref[at(i), :])
            out_ref[at(i), :] = (hat * norm_ref[2:3, :] + norm_ref[3:4, :]).astype(bf16)
            grad = og_ref[at(i), :].astype(f32)
            back, g, b = layer_norm_back(grad, hat, scale, norm_ref[2:3, :])
            gain = g if i == 0 else gain + g
            bias = b if i == 0 else bias + b
            acc_ref[at(i), :] = back
            fgrad_ref[at(i), :] = back.astype(bf16)
        small_ref[2:3, :] = gain
        small_ref[3:4, :] = bias

    @pl.when(step >= chunks)
    def _():
        j = step - chunks
        slot = lax.rem(j, 2)

        @pl.when(j >= 2)
        def _():
            for copy in copies(j - 2):
                copy.wait()

        for i in range(blocks):
            hidden_grad = dot_nt(fgrad_ref[at(i), :], wd_ref[...])
            gg = (hidden_grad * b_ref[j, at(i), :].astype(f32)).astype(bf16)
            ug = (hidden_grad * a_ref[j, at(i), :].astype(f32)).astype(bf16)
            gg_ref[at(i), :] = gg
            ug_ref[at(i), :] = ug
            acc_ref[at(i), :] += dot_nt(gg, wg_ref[...]) + dot_nt(ug, wu_ref[...])
        stage_g[slot] = dot_nn(ylowt_ref[...], gg_ref[...]).astype(bf16)
        stage_u[slot] = dot_nn(ylowt_ref[...], ug_ref[...]).astype(bf16)
        stage_d[slot] = dot_tn(h_ref[j], fgrad_ref[...]).astype(bf16)
        for copy in copies(j):
            copy.start()

    @pl.when(step == 2 * chunks - 1)
    def _():
        gain = bias = None
        for i in range(blocks):
            back, g, b = layer_norm_back(acc_ref[at(i), :], hat_ref[at(i), :], scale_ref[at(i), :], norm_ref[0:1, :])
            gain = g if i == 0 else gain + g
            bias = b if i == 0 else bias + b
            first_ref[at(i), :] = back
            low = back.astype(bf16)
            fgrad_ref[at(i), :] = low
            ograd_ref[at(i), :] = dot_nt(low, wo_ref[...]).astype(bf16)
        small_ref[0:1, :] = gain
        small_ref[1:2, :] = bias
        small_ref[4:8, :] = jnp.zeros((4, width), f32)
        stage_o[...] = dot_tn(o_ref[...], fgrad_ref[...]).astype(bf16)
        last = pltpu.make_async_copy(stage_o, grads_ref.at[:, pl.ds(0, width)], sems.at[2, 0])
        last.start()
        for j in (chunks - 2, chunks - 1):
            for copy in copies(j):
                copy.wait()
        last.wait()


def feed_forward(o, x, out_grad, w_rest, norms):
    rows, width = x.shape
    chunks = FF // CHUNK
    lead = width // CHUNK
    per = width // CHUNK

    def whole(shape):
        return pl.BlockSpec(shape, lambda s: (0,) * len(shape), pipeline_mode=pl.Buffered(1))

    full = whole((rows, width))
    return pl.pallas_call(
        ffn_kernel,
        grid=(2 * chunks,),
        in_specs=[
            full, full, full,
            whole((width, width)),
            pl.BlockSpec((width, CHUNK), lambda s: (0, lead + lax.rem(s, chunks))),
            pl.BlockSpec((width, CHUNK), lambda s: (0, lead + chunks + lax.rem(s, chunks))),
            pl.BlockSpec((CHUNK, width), lambda s: (lax.rem(lax.rem(s, chunks), per), 1 + 2 * FF // width + lax.div(lax.rem(s, chunks), per))),
            whole(norms.shape),
        ],
        out_specs=[full, full, full, whole((8, width)), pl.BlockSpec(memory_space=pl.ANY)],
        out_shape=[
            jax.ShapeDtypeStruct((rows, width), bf16),
            jax.ShapeDtypeStruct((rows, width), f32),
            jax.ShapeDtypeStruct((rows, width), bf16),
            jax.ShapeDtypeStruct((8, width), f32),
            jax.ShapeDtypeStruct((width, w_rest.shape[1]), bf16),
        ],
        scratch_shapes=[
            pltpu.VMEM((rows, width), f32),
            pltpu.VMEM((rows, 1), f32),
            pltpu.VMEM((rows, width), f32),
            pltpu.VMEM((chunks, rows, CHUNK), bf16),
            pltpu.VMEM((chunks, rows, CHUNK), bf16),
            pltpu.VMEM((chunks, rows, CHUNK), bf16),
            pltpu.VMEM((rows, width), bf16),
            pltpu.VMEM((width, rows), bf16),
            pltpu.VMEM((rows, width), bf16),
            pltpu.VMEM((rows, CHUNK), bf16),
            pltpu.VMEM((rows, CHUNK), bf16),
            pltpu.VMEM((2, width, CHUNK), bf16),
            pltpu.VMEM((2, width, CHUNK), bf16),
            pltpu.VMEM((2, CHUNK, width), bf16),
            pltpu.VMEM((width, width), bf16),
            pltpu.SemaphoreType.DMA((3, 3)),
        ],
        compiler_params=pltpu.CompilerParams(vmem_limit_bytes=58 * 2**20),
        cost_estimate=pl.CostEstimate(flops=46 * 10**9, bytes_accessed=6 * 10**7, transcendentals=6 * 10**6),
        name="feed_forward",
    )(o, x, out_grad, w_rest, w_rest, w_rest, w_rest, norms)


def on_device(inputs, out_grad, segments, windows, owners, weights, first_moments, second_moments,
              norm_params, norm_first, norm_second):
    seqs, tokens, width = inputs.shape
    rows = seqs * tokens
    heads = windows.shape[0]
    slots = weights.shape[0]
    owner_count = lax.axis_size("seq")
    me = lax.axis_index("seq")
    seq_len = segments.shape[1]
    keys = tokens + 2 * REACH
    pieces = REACH // tokens
    groups = FF // width
    units = owners.shape[0]
    rest = units - 3

    ids = jnp.arange(units, dtype=jnp.int32)
    before = (owners[None, :] == owners[:, None]) & (ids[None, :] < ids[:, None])
    rank = jnp.sum(before.astype(jnp.int32), axis=1)
    slot_ids = jnp.arange(owner_count * slots, dtype=jnp.int32)
    match = (owners * slots + rank)[None, :] == slot_ids[:, None]
    unit_of = jnp.max(jnp.where(match, ids[None, :], -1), axis=1)
    my_units = lax.dynamic_slice_in_dim(unit_of, me * slots, slots, 0)

    left = [shifted(inputs, "ctx", pieces - n) for n in range(pieces)]
    right = [shifted(inputs, "ctx", -(n + 1)) for n in range(pieces)]

    low = weights.astype(bf16)
    if owner_count == 2:
        place = jnp.stack([jnp.where(owners == me, 0, 1), rank])
        own_first = pick_units(place[:, :3] * jnp.array([[0], [1]], jnp.int32), [low], 3)
        got_first = swapped(own_first, "seq", 1)
        mine = jnp.repeat(owners[:3] == me, width)[None, :]
        picked_first = jnp.where(mine, own_first, got_first)
        sources = [low, swapped(low, "seq", 1)]
    else:
        every = lax.all_gather(low, "seq", axis=0, tiled=True)
        place = jnp.stack([jnp.zeros_like(owners), owners * slots + rank])
        sources = [every]
        picked_first = pick_units(place[:, :3], sources, 3)
    w_first = lax.all_gather(picked_first, "ctx", axis=0, tiled=True)
    picked_rest = pick_units(place[:, 3:], sources, rest)
    picked_rest, w_first, left, right = lax.optimization_barrier((picked_rest, w_first, left, right))
    w_rest = lax.all_gather(picked_rest, "ctx", axis=0, tiled=True)

    start = lax.axis_index("ctx") * tokens
    padded = jnp.pad(segments, ((0, 0), (REACH, 0)), constant_values=-1)
    padded = jnp.pad(padded, ((0, 0), (0, REACH)), constant_values=1 << 20)
    key_seg = lax.dynamic_slice_in_dim(padded, start, keys, 1)
    query_seg = key_seg[:, REACH : REACH + tokens]
    lo = jnp.sum((key_seg[:, :, None] < query_seg[:, None, :]).astype(jnp.int32), axis=1)[:, None]
    hi = jnp.sum((key_seg[:, :, None] <= query_seg[:, None, :]).astype(jnp.int32), axis=1)[:, None] - 1
    slopes2 = jnp.power(2.0, -8.0 * (jnp.arange(heads, dtype=f32) + 1.0) / heads) * LOG2E

    x_ext = jnp.concatenate(left + [inputs] + right, axis=1)
    w_q, w_kv = w_first[:, :width], w_first[:, width:]
    x = inputs.reshape(rows, width)
    q = dot_nn(x, w_q).astype(bf16).reshape(seqs, tokens, width)
    kv = dot_nn(x_ext.reshape(seqs * keys, width), w_kv).astype(bf16).reshape(seqs, keys, 2 * width)
    mixed, lse, peaks = attend_fwd(windows, slopes2, q, kv, lo, hi)
    peak = jnp.max(peaks, axis=(1, 2))
    o = mixed.reshape(rows, width)

    result, first_grad, o_grad, small, rest_grads = feed_forward(
        o, x, out_grad.reshape(rows, width), w_rest, norm_params
    )
    output = result.reshape(seqs, tokens, width)
    rest_sums = lax.psum_scatter(rest_grads, "ctx", scatter_dimension=0, tiled=True)
    dq, dk, dv = attend_bwd(windows, slopes2, q, kv, o_grad.reshape(seqs, tokens, width), mixed, lo, hi, lse)

    xe = x_ext.reshape(seqs * keys, width)
    dk_flat, dv_flat = dk.reshape(seqs * keys, width), dv.reshape(seqs * keys, width)
    first_grads = jnp.concatenate(
        [dot_tn(x, dq.reshape(rows, width)).astype(bf16), dot_tn(xe, dk_flat).astype(bf16), dot_tn(xe, dv_flat).astype(bf16)],
        axis=1,
    )
    first_sums = exchange_scatter(first_grads, "ctx")

    key_part = (dot_nt(dk_flat, w_kv[:, :width]) + dot_nt(dv_flat, w_kv[:, width:])).reshape(seqs, keys, width)
    input_grad = first_grad.reshape(seqs, tokens, width) + dot_nt(dq.reshape(rows, width), w_q).reshape(seqs, tokens, width)
    input_grad = input_grad + key_part[:, REACH : REACH + tokens]
    for n in range(pieces):
        to_left = key_part[:, n * tokens : (n + 1) * tokens].astype(bf16)
        to_right = key_part[:, REACH + (n + 1) * tokens : REACH + (n + 2) * tokens].astype(bf16)
        input_grad = input_grad + shifted(to_left, "ctx", n - pieces).astype(f32)
        input_grad = input_grad + shifted(to_right, "ctx", n + 1).astype(f32)

    is_peak_row = (jnp.arange(8) == 4)[:, None]
    small = jnp.where(is_peak_row, jnp.pad(peak, (0, width - heads))[None], small)
    for axis in ("ctx", "seq"):
        bit = 1
        while bit < lax.axis_size(axis):
            other = swapped(small, axis, bit)
            small = jnp.where(is_peak_row, jnp.maximum(small, other), small + other)
            bit *= 2
    norm_grads = small[:4]
    factors = clip_level / jnp.maximum(small[4, :heads], clip_level)
    column_scale = jnp.repeat(jnp.sqrt(factors), width // heads)[None, :]
    correction = 1.0 - 0.5**STEP

    def owned(columns, lowest):
        count = columns.shape[1] // width
        local = unit_of - lowest
        local = jnp.where((local >= 0) & (local < count), local, -1)
        if owner_count == 2:
            keep = to_slots(lax.dynamic_slice_in_dim(local, me * slots, slots, 0), columns, slots, width)
            give = to_slots(lax.dynamic_slice_in_dim(local, (1 - me) * slots, slots, 0), columns, slots, width)
            return [keep, swapped(give, "seq", 1)]
        every = to_slots(local, columns, owner_count * slots, width)
        return [lax.psum_scatter(every, "seq", scatter_dimension=0, tiled=True)]

    parts = owned(rest_sums, 3) + owned(first_sums, 0)
    weight_grads, new_weights, new_first, new_second, weights_low = adam_slots(
        my_units, weights, first_moments, second_moments, parts, column_scale, correction, 0.5 / D**0.5
    )
    new_norms, new_norm_first, new_norm_second = adam_step(
        norm_params, norm_grads, norm_first, norm_second, correction, norm_rate
    )
    return (output, input_grad, weight_grads, norm_grads, new_weights, new_first, new_second, weights_low,
            new_norms, new_norm_first, new_norm_second, factors)


def solution(mesh):
    block = P("seq", "ctx", None)
    return jax.shard_map(
        on_device,
        mesh=mesh,
        in_specs=(block, block, P("seq", None), P(), P(), block, block, block, P(), P(), P()),
        out_specs=(block, block, block, P(), block, block, block, block, P(), P(), P(), P()),
        check_vma=False,
    )
```

```python
import jax
import jax.numpy as jnp
from jax import lax
from jax.experimental import pallas as pl
from jax.experimental.pallas import tpu as pltpu
from jax.sharding import PartitionSpec as P

D = 768
FF = 3072
STEP = 3
clip_level = 1.0
decay_rate = 0.1
norm_rate = 0.25
LOG2E = 1.4426950408889634
NEG = -1e30
REACH = 512
QB = 256
bf16 = jnp.bfloat16
f32 = jnp.float32

def dot_nt(a, b):
    return lax.dot_general(a, b, (((1,), (1,)), ((), ())), preferred_element_type=f32)

def dot_nn(a, b):
    return lax.dot_general(a, b, (((1,), (0,)), ((), ())), preferred_element_type=f32)

def fill_bias(bias_ref, slope2):
    rows = bias_ref.shape[0]
    k = lax.broadcasted_iota(jnp.int32, (rows, QB), 0)
    q = lax.broadcasted_iota(jnp.int32, (rows, QB), 1)
    bias_ref[...] = jnp.abs(k - q - REACH).astype(f32) * (-slope2)

def fold8(x, op):
    y = x.reshape(x.shape[0] // 8, 8, x.shape[1])
    return op(y, axis=0)

def head_window(win_ref, lo_ref, hi_ref, head, qb):
    reach = (win_ref[head] - 1) >> 1
    cls = jnp.clip((reach + 127) >> 7, 2, 4)
    qpos = lax.broadcasted_iota(jnp.int32, (1, QB), 1) + (qb * QB + REACH)
    lo = jnp.maximum(lo_ref[0, :, pl.ds(qb * QB, QB)], qpos - reach)
    hi = jnp.minimum(hi_ref[0, :, pl.ds(qb * QB, QB)], qpos + reach)
    return cls, lo, hi

def fwd_kernel(win_ref, slope_ref, q_ref, k_ref, v_ref, lo_ref, hi_ref, o_ref, lse_ref, peak_ref,
               vt_ref, ot_ref, z_ref, bias_ref):
    pair = pl.program_id(0)
    seq = pl.program_id(1)
    tokens = q_ref.shape[1]
    vt_ref[...] = v_ref[0].T

    @pl.when(seq == 0)
    def _():
        peak_ref[...] = jnp.full(peak_ref.shape, NEG, f32)

    rows = lax.broadcasted_iota(jnp.int32, (QB, QB), 0)
    lane = lax.broadcasted_iota(jnp.int32, (1, 128), 1)
    for h in range(2):
        head = pair * 2 + h
        @pl.when(seq == 0)
        def _():
            fill_bias(bias_ref.at[h], slope_ref[head])
        hmask = jnp.where((lane >= h * 64) & (lane < h * 64 + 64), 0.125, 0.0)
        for qb in range(tokens // QB):
            cls, lo, hi = head_window(win_ref, lo_ref, hi_ref, head, qb)
            q = (q_ref[0, pl.ds(qb * QB, QB), :].astype(f32) * hmask).astype(bf16)

            def branch(c):
                reach = c * 128
                first = REACH - reach
                n = 1 + c
                pk = mx = None
                for t in range(n):
                    b = first + t * QB
                    s = dot_nt(k_ref[0, pl.ds(qb * QB + b, QB), :], q)
                    kk = rows + (qb * QB + b)
                    s = jnp.where((kk >= lo) & (kk <= hi), s, NEG)
                    z = s * LOG2E + bias_ref[h, pl.ds(b, QB), :]
                    a, d = fold8(s, jnp.max), fold8(z, jnp.max)
                    pk = a if t == 0 else jnp.maximum(pk, a)
                    mx = d if t == 0 else jnp.maximum(mx, d)
                    z_ref[pl.ds(t * QB, QB), :] = z
                peak_ref[h] = jnp.maximum(peak_ref[h], pk)
                m = jnp.max(mx, axis=0, keepdims=True)
                acc = total = None
                for t in range(n):
                    p = jnp.exp2(z_ref[pl.ds(t * QB, QB), :] - m)
                    e = fold8(p, jnp.sum)
                    total = e if t == 0 else total + e
                    b = first + t * QB
                    part = dot_nn(vt_ref[pl.ds(h * 64, 64), pl.ds(qb * QB + b, QB)], p.astype(bf16))
                    acc = part if t == 0 else acc + part
                total = jnp.sum(total, axis=0, keepdims=True)
                ot_ref[pl.ds(h * 64, 64), pl.ds(qb * QB, QB)] = acc * (1.0 / total)
                lse_ref[0, 0, pl.ds(h, 1), pl.ds(qb * QB, QB)] = m + jnp.log2(total)

            for c in (2, 3, 4):
                pl.when(cls == c)(lambda c=c: branch(c))
    o_ref[0] = ot_ref[...].T.astype(bf16)

def attend_fwd(windows, slopes2, q, kv, lo, hi):
    seqs, tokens, width = q.shape
    keys = kv.shape[1]
    pairs = width // 128
    smem = pl.BlockSpec(memory_space=pltpu.SMEM)
    return pl.pallas_call(
        fwd_kernel,
        grid=(pairs, seqs),
        in_specs=[
            smem, smem,
            pl.BlockSpec((1, tokens, 128), lambda p, s: (s, 0, p)),
            pl.BlockSpec((1, keys, 128), lambda p, s: (s, 0, p)),
            pl.BlockSpec((1, keys, 128), lambda p, s: (s, 0, p + pairs)),
            pl.BlockSpec((1, 1, tokens), lambda p, s: (s, 0, 0)),
            pl.BlockSpec((1, 1, tokens), lambda p, s: (s, 0, 0)),
        ],
        out_specs=[
            pl.BlockSpec((1, tokens, 128), lambda p, s: (s, 0, p)),
            pl.BlockSpec((1, 1, 2, tokens), lambda p, s: (s, p, 0, 0)),
            pl.BlockSpec((2, 8, QB), lambda p, s: (p, 0, 0)),
        ],
        out_shape=[
            jax.ShapeDtypeStruct((seqs, tokens, width), bf16),
            jax.ShapeDtypeStruct((seqs, pairs, 2, tokens), f32),
            jax.ShapeDtypeStruct((2 * pairs, 8, QB), f32),
        ],
        scratch_shapes=[
            pltpu.VMEM((128, keys), bf16),
            pltpu.VMEM((128, tokens), f32),
            pltpu.VMEM((QB + 2 * REACH, QB), f32),
            pltpu.VMEM((2, QB + 2 * REACH, QB), f32),
        ],
        compiler_params=pltpu.CompilerParams(vmem_limit_bytes=40 * 2**20),
        cost_estimate=pl.CostEstimate(flops=2 * 10**10, bytes_accessed=10**7, transcendentals=10**7),
        name="attend_fwd",
    )(windows, slopes2, q, kv, kv, lo, hi)

def bwd_kernel(win_ref, slope_ref, q_ref, k_ref, v_ref, do_ref, o_ref, lo_ref, hi_ref, lse_ref,
               dq_ref, dk_ref, dv_ref, kt_ref, dqt_ref, dka_ref, dva_ref, bias_ref):
    pair = pl.program_id(0)
    seq = pl.program_id(1)
    tokens = q_ref.shape[1]
    kt_ref[...] = k_ref[0].T
    dka_ref[...] = jnp.zeros(dka_ref.shape, f32)
    dva_ref[...] = jnp.zeros(dva_ref.shape, f32)
    rows = lax.broadcasted_iota(jnp.int32, (QB, QB), 0)
    lane = lax.broadcasted_iota(jnp.int32, (1, 128), 1)
    ones = jnp.ones((16, 128), bf16)
    for h in range(2):
        head = pair * 2 + h
        @pl.when(seq == 0)
        def _():
            fill_bias(bias_ref.at[h], slope_ref[head])
        inside = (lane >= h * 64) & (lane < h * 64 + 64)
        qmask = jnp.where(inside, 0.125, 0.0)
        dmask = jnp.where(inside, 1.0, 0.0)
        for qb in range(tokens // QB):
            cls, lo, hi = head_window(win_ref, lo_ref, hi_ref, head, qb)
            q = (q_ref[0, pl.ds(qb * QB, QB), :].astype(f32) * qmask).astype(bf16)
            do = (do_ref[0, pl.ds(qb * QB, QB), :].astype(f32) * dmask).astype(bf16)
            lse = lse_ref[0, 0, pl.ds(h, 1), pl.ds(qb * QB, QB)]
            prod = do.astype(f32) * o_ref[0, pl.ds(qb * QB, QB), :].astype(f32)
            prod_hi = prod.astype(bf16)
            prod_lo = (prod - prod_hi.astype(f32)).astype(bf16)
            dsum = (dot_nt(ones, prod_hi) + dot_nt(ones, prod_lo))[:1]

            def branch(c):
                first = REACH - c * 128
                dqt = None
                for t in range(1 + c):
                    b = first + t * QB
                    at = pl.ds(qb * QB + b, QB)
                    s = dot_nt(k_ref[0, at, :], q)
                    dp = dot_nt(v_ref[0, at, :], do)
                    kk = rows + (qb * QB + b)
                    z = s * LOG2E + (bias_ref[h, pl.ds(b, QB), :] - lse)
                    p = jnp.exp2(jnp.where((kk >= lo) & (kk <= hi), z, NEG))
                    ds = (p * (dp - dsum)).astype(bf16)
                    dva_ref[at, :] += dot_nn(p.astype(bf16), do)
                    dka_ref[at, :] += dot_nn(ds, q)
                    part = dot_nn(kt_ref[pl.ds(h * 64, 64), at], ds)
                    dqt = part if t == 0 else dqt + part
                dqt_ref[pl.ds(h * 64, 64), pl.ds(qb * QB, QB)] = dqt * 0.125

            for c in (2, 3, 4):
                pl.when(cls == c)(lambda c=c: branch(c))
    dq_ref[0] = dqt_ref[...].T.astype(bf16)
    dk_ref[0] = dka_ref[...].astype(bf16)
    dv_ref[0] = dva_ref[...].astype(bf16)

def attend_bwd(windows, slopes2, q, kv, do, o, lo, hi, lse):
    seqs, tokens, width = q.shape
    keys = kv.shape[1]
    pairs = width // 128
    smem = pl.BlockSpec(memory_space=pltpu.SMEM)
    tok = pl.BlockSpec((1, tokens, 128), lambda p, s: (s, 0, p))
    key = pl.BlockSpec((1, keys, 128), lambda p, s: (s, 0, p))
    row = pl.BlockSpec((1, 1, tokens), lambda p, s: (s, 0, 0))
    stat = pl.BlockSpec((1, 1, 2, tokens), lambda p, s: (s, p, 0, 0))
    return pl.pallas_call(
        bwd_kernel,
        grid=(pairs, seqs),
        in_specs=[smem, smem, tok, key, pl.BlockSpec((1, keys, 128), lambda p, s: (s, 0, p + pairs)), tok, tok, row, row, stat],
        out_specs=[tok, key, key],
        out_shape=[
            jax.ShapeDtypeStruct((seqs, tokens, width), bf16),
            jax.ShapeDtypeStruct((seqs, keys, width), bf16),
            jax.ShapeDtypeStruct((seqs, keys, width), bf16),
        ],
        scratch_shapes=[
            pltpu.VMEM((128, keys), bf16),
            pltpu.VMEM((128, tokens), f32),
            pltpu.VMEM((keys, 128), f32),
            pltpu.VMEM((keys, 128), f32),
            pltpu.VMEM((2, QB + 2 * REACH, QB), f32),
        ],
        compiler_params=pltpu.CompilerParams(vmem_limit_bytes=40 * 2**20),
        cost_estimate=pl.CostEstimate(flops=5 * 10**10, bytes_accessed=2 * 10**7, transcendentals=10**7),
        name="attend_bwd",
    )(windows, slopes2, q, kv, kv, do, o, lo, hi, lse)

def shifted(value, axis, by):
    peers = lax.axis_size(axis)
    pairs = [(i, i + by) for i in range(peers) if 0 <= i + by < peers]
    return lax.ppermute(value, axis, pairs)


def swapped(value, axis, bit):
    peers = lax.axis_size(axis)
    return lax.ppermute(value, axis, [(i, i ^ bit) for i in range(peers)])


def layer_norm(rows_in):
    center = rows_in - jnp.mean(rows_in, axis=-1, keepdims=True)
    spread = jnp.mean(center * center, axis=-1, keepdims=True)
    scale = lax.rsqrt(spread + 1e-05)
    return center * scale, scale


def layer_norm_back(grad, hat, scale, gain):
    inner = grad * gain
    mean_one = jnp.mean(inner, axis=-1, keepdims=True)
    mean_two = jnp.mean(inner * hat, axis=-1, keepdims=True)
    back = scale * (inner - mean_one - hat * mean_two)
    return back, jnp.sum(grad * hat, axis=0, keepdims=True), jnp.sum(grad, axis=0, keepdims=True)


def halve(value, axis, bit, dim):
    side = (lax.axis_index(axis) // bit) % 2
    keep = lax.dynamic_index_in_dim(value, side, dim, False)
    got = swapped(lax.dynamic_index_in_dim(value, 1 - side, dim, False), axis, bit)
    return (keep.astype(f32) + got.astype(f32)).astype(value.dtype)


def pick_units(slot_of, sources, count, pad=0):
    slots, rows, width = sources[0].shape

    def kernel(slot_ref, *refs):
        out_ref = refs[-1]
        if pad:
            out_ref[:, pl.ds(count * width, pad)] = jnp.zeros((rows, pad), out_ref.dtype)
        for u in range(count):
            at = pl.ds(u * width, width)
            for number, ref in enumerate(refs[:-1]):

                @pl.when(slot_ref[0, u] == number)
                def _(ref=ref, u=u, at=at):
                    out_ref[:, at] = ref[slot_ref[1, u]]

    vmem = pl.BlockSpec(memory_space=pltpu.VMEM)
    return pl.pallas_call(
        kernel,
        in_specs=[pl.BlockSpec(memory_space=pltpu.SMEM)] + [vmem] * len(sources),
        out_specs=vmem,
        out_shape=jax.ShapeDtypeStruct((rows, count * width + pad), sources[0].dtype),
        compiler_params=pltpu.CompilerParams(vmem_limit_bytes=24 * 2**20),
        name="pick_units",
    )(slot_of, *sources)


def to_slots(unit_of, columns, slots, width):
    rows = columns.shape[0]

    def kernel(unit_ref, col_ref, out_ref):
        for s in range(slots):
            unit = unit_ref[s]

            @pl.when(unit >= 0)
            def _(s=s, unit=unit):
                out_ref[s] = col_ref[:, pl.ds(pl.multiple_of(unit * width, 128), width)]

            @pl.when(unit < 0)
            def _(s=s):
                out_ref[s] = jnp.zeros((rows, width), out_ref.dtype)

    vmem = pl.BlockSpec(memory_space=pltpu.VMEM)
    return pl.pallas_call(
        kernel,
        in_specs=[pl.BlockSpec(memory_space=pltpu.SMEM), vmem],
        out_specs=vmem,
        out_shape=jax.ShapeDtypeStruct((slots, rows, width), columns.dtype),
        compiler_params=pltpu.CompilerParams(vmem_limit_bytes=24 * 2**20),
        name="to_slots",
    )(unit_of, columns)


def adam_slots(unit_of, weights, first, second, grads, scale, correction, rate):
    slots, rows, width = weights.shape

    def kernel(unit_ref, w_ref, m_ref, v_ref, scale_ref, *refs):
        grad_refs, (g_out, w_out, m_out, v_out, low_out) = refs[:-5], refs[-5:]
        unit = unit_ref[pl.program_id(0)]
        live = unit >= 0
        g = grad_refs[0][0].astype(f32)
        for ref in grad_refs[1:]:
            g = g + ref[0].astype(f32)
        g = jnp.where(live, g, 0.0)
        w = w_ref[0]
        m = 0.5 * m_ref[0] + 0.5 * g
        v = 0.5 * v_ref[0] + 0.5 * g * g
        step = m * (1.0 / correction) / (jnp.sqrt(v * (1.0 / correction)) + 1e-08)
        moved = w - rate * (step + decay_rate * w)
        moved = jnp.where((unit == 0) | (unit == 1), moved * scale_ref[...], moved)
        moved = jnp.where(live, moved, 0.0)
        g_out[0] = g
        w_out[0] = moved
        m_out[0] = jnp.where(live, m, 0.0)
        v_out[0] = jnp.where(live, v, 0.0)
        low_out[0] = moved.astype(bf16)

    block = pl.BlockSpec((1, rows, width), lambda s: (s, 0, 0))
    wide = jax.ShapeDtypeStruct(weights.shape, f32)
    return pl.pallas_call(
        kernel,
        grid=(slots,),
        in_specs=[pl.BlockSpec(memory_space=pltpu.SMEM), block, block, block,
                  pl.BlockSpec((1, width), lambda s: (0, 0))] + [block] * len(grads),
        out_specs=[block] * 5,
        out_shape=[wide] * 4 + [jax.ShapeDtypeStruct(weights.shape, bf16)],
        compiler_params=pltpu.CompilerParams(vmem_limit_bytes=24 * 2**20),
        name="adam_slots",
    )(unit_of, weights, first, second, scale, *grads)


def adam_step(master, gradient, first, second, correction, learn_rate):
    new_first = 0.5 * first + 0.5 * gradient
    new_second = 0.5 * second + 0.5 * gradient * gradient
    normed = new_first / correction / (jnp.sqrt(new_second / correction) + 1e-08)
    return (master - learn_rate * (normed + decay_rate * master), new_first, new_second)


def dot_tn(a, b):
    return lax.dot_general(a, b, (((0,), (0,)), ((), ())), preferred_element_type=f32)


def gelu_parts(gate):
    cdf = 0.5 * (1.0 + lax.erf(gate * 0.7071067811865476))
    density = 0.3989422804014327 * jnp.exp(-0.5 * gate * gate)
    return cdf, density


RB = 512
CHUNK = 256


def ffn_kernel(o_ref, x_ref, og_ref, wo_ref, wg_ref, wu_ref, wd_ref, norm_ref,
               out_ref, first_ref, ograd_ref, small_ref, grads_ref,
               hat_ref, scale_ref, acc_ref, a_ref, b_ref, h_ref, ylow_ref, ylowt_ref, fgrad_ref,
               gg_ref, ug_ref, stage_g, stage_u, stage_d, stage_o, sems):
    step = pl.program_id(0)
    rows, width = x_ref.shape
    chunk = wg_ref.shape[1]
    chunks = FF // chunk
    blocks = rows // RB

    def at(i):
        return pl.ds(i * RB, RB)

    def copies(j):
        slot = lax.rem(j, 2)
        column = pl.multiple_of(width + j * chunk, 128)
        per = width // chunk
        return (
            pltpu.make_async_copy(stage_g.at[slot], grads_ref.at[:, pl.ds(column, chunk)], sems.at[slot, 0]),
            pltpu.make_async_copy(stage_u.at[slot], grads_ref.at[:, pl.ds(column + FF, chunk)], sems.at[slot, 1]),
            pltpu.make_async_copy(
                stage_d.at[slot],
                grads_ref.at[pl.ds(pl.multiple_of(lax.rem(j, per) * chunk, 128), chunk),
                             pl.ds(pl.multiple_of(width + 2 * FF + lax.div(j, per) * width, 128), width)],
                sems.at[slot, 2],
            ),
        )

    @pl.when(step == 0)
    def _():
        for i in range(blocks):
            total = x_ref[at(i), :].astype(f32) + dot_nn(o_ref[at(i), :], wo_ref[...])
            hat, scale = layer_norm(total)
            y1 = hat * norm_ref[0:1, :] + norm_ref[1:2, :]
            hat_ref[at(i), :] = hat
            scale_ref[at(i), :] = scale
            acc_ref[at(i), :] = y1
            ylow_ref[at(i), :] = y1.astype(bf16)
            ylowt_ref[:, at(i)] = y1.T.astype(bf16)

    @pl.when(step < chunks)
    def _():
        for i in range(blocks):
            y = ylow_ref[at(i), :]
            gate = dot_nn(y, wg_ref[...])
            up = dot_nn(y, wu_ref[...])
            cdf, density = gelu_parts(gate)
            a = gate * cdf
            hidden = (a * up).astype(bf16)
            a_ref[step, at(i), :] = a.astype(bf16)
            b_ref[step, at(i), :] = (up * (cdf + gate * density)).astype(bf16)
            h_ref[step, at(i), :] = hidden
            acc_ref[at(i), :] += dot_nn(hidden, wd_ref[...])

    @pl.when(step == chunks)
    def _():
        gain = bias = None
        for i in range(blocks):
            hat, scale = layer_norm(acc_ref[at(i), :])
            out_ref[at(i), :] = (hat * norm_ref[2:3, :] + norm_ref[3:4, :]).astype(bf16)
            grad = og_ref[at(i), :].astype(f32)
            back, g, b = layer_norm_back(grad, hat, scale, norm_ref[2:3, :])
            gain = g if i == 0 else gain + g
            bias = b if i == 0 else bias + b
            acc_ref[at(i), :] = back
            fgrad_ref[at(i), :] = back.astype(bf16)
        small_ref[2:3, :] = gain
        small_ref[3:4, :] = bias

    @pl.when(step >= chunks)
    def _():
        j = step - chunks
        slot = lax.rem(j, 2)

        @pl.when(j >= 2)
        def _():
            for copy in copies(j - 2):
                copy.wait()

        for i in range(blocks):
            hidden_grad = dot_nt(fgrad_ref[at(i), :], wd_ref[...])
            gg = (hidden_grad * b_ref[j, at(i), :].astype(f32)).astype(bf16)
            ug = (hidden_grad * a_ref[j, at(i), :].astype(f32)).astype(bf16)
            gg_ref[at(i), :] = gg
            ug_ref[at(i), :] = ug
            acc_ref[at(i), :] += dot_nt(gg, wg_ref[...]) + dot_nt(ug, wu_ref[...])
        stage_g[slot] = dot_nn(ylowt_ref[...], gg_ref[...]).astype(bf16)
        stage_u[slot] = dot_nn(ylowt_ref[...], ug_ref[...]).astype(bf16)
        stage_d[slot] = dot_tn(h_ref[j], fgrad_ref[...]).astype(bf16)
        for copy in copies(j):
            copy.start()

    @pl.when(step == 2 * chunks - 1)
    def _():
        gain = bias = None
        for i in range(blocks):
            back, g, b = layer_norm_back(acc_ref[at(i), :], hat_ref[at(i), :], scale_ref[at(i), :], norm_ref[0:1, :])
            gain = g if i == 0 else gain + g
            bias = b if i == 0 else bias + b
            first_ref[at(i), :] = back
            low = back.astype(bf16)
            fgrad_ref[at(i), :] = low
            ograd_ref[at(i), :] = dot_nt(low, wo_ref[...]).astype(bf16)
        small_ref[0:1, :] = gain
        small_ref[1:2, :] = bias
        small_ref[4:8, :] = jnp.zeros((4, width), f32)
        stage_o[...] = dot_tn(o_ref[...], fgrad_ref[...]).astype(bf16)
        last = pltpu.make_async_copy(stage_o, grads_ref.at[:, pl.ds(0, width)], sems.at[2, 0])
        last.start()
        for j in (chunks - 2, chunks - 1):
            for copy in copies(j):
                copy.wait()
        last.wait()


def feed_forward(o, x, out_grad, w_rest, norms):
    rows, width = x.shape
    chunks = FF // CHUNK
    lead = width // CHUNK
    per = width // CHUNK

    def whole(shape):
        return pl.BlockSpec(shape, lambda s: (0,) * len(shape), pipeline_mode=pl.Buffered(1))

    full = whole((rows, width))
    return pl.pallas_call(
        ffn_kernel,
        grid=(2 * chunks,),
        in_specs=[
            full, full, full,
            whole((width, width)),
            pl.BlockSpec((width, CHUNK), lambda s: (0, lead + lax.rem(s, chunks))),
            pl.BlockSpec((width, CHUNK), lambda s: (0, lead + chunks + lax.rem(s, chunks))),
            pl.BlockSpec((CHUNK, width), lambda s: (lax.rem(lax.rem(s, chunks), per), 1 + 2 * FF // width + lax.div(lax.rem(s, chunks), per))),
            whole(norms.shape),
        ],
        out_specs=[full, full, full, whole((8, width)), pl.BlockSpec(memory_space=pl.ANY)],
        out_shape=[
            jax.ShapeDtypeStruct((rows, width), bf16),
            jax.ShapeDtypeStruct((rows, width), f32),
            jax.ShapeDtypeStruct((rows, width), bf16),
            jax.ShapeDtypeStruct((8, width), f32),
            jax.ShapeDtypeStruct((width, width + 3 * FF), bf16),
        ],
        scratch_shapes=[
            pltpu.VMEM((rows, width), f32),
            pltpu.VMEM((rows, 1), f32),
            pltpu.VMEM((rows, width), f32),
            pltpu.VMEM((chunks, rows, CHUNK), bf16),
            pltpu.VMEM((chunks, rows, CHUNK), bf16),
            pltpu.VMEM((chunks, rows, CHUNK), bf16),
            pltpu.VMEM((rows, width), bf16),
            pltpu.VMEM((width, rows), bf16),
            pltpu.VMEM((rows, width), bf16),
            pltpu.VMEM((rows, CHUNK), bf16),
            pltpu.VMEM((rows, CHUNK), bf16),
            pltpu.VMEM((2, width, CHUNK), bf16),
            pltpu.VMEM((2, width, CHUNK), bf16),
            pltpu.VMEM((2, CHUNK, width), bf16),
            pltpu.VMEM((width, width), bf16),
            pltpu.SemaphoreType.DMA((3, 3)),
        ],
        compiler_params=pltpu.CompilerParams(vmem_limit_bytes=58 * 2**20),
        cost_estimate=pl.CostEstimate(flops=46 * 10**9, bytes_accessed=6 * 10**7, transcendentals=6 * 10**6),
        name="feed_forward",
    )(o, x, out_grad, w_rest, w_rest, w_rest, w_rest, norms)

def first_gradients(x_t, dq, dk, dv, tokens):
    width, total = x_t.shape
    seqs = dq.shape[0] // tokens
    keys = total // seqs
    cols = 256
    per = width // cols

    def kernel(x_ref, q_ref, k_ref, v_ref, out_ref):
        unit = pl.program_id(0)

        @pl.when(unit == 0)
        def _():
            acc = None
            for s in range(seqs):
                part = dot_nn(x_ref[:, pl.ds(s * keys + REACH, tokens)], q_ref[pl.ds(s * tokens, tokens), :])
                acc = part if s == 0 else acc + part
            out_ref[...] = acc.astype(bf16)

        @pl.when(unit == 1)
        def _():
            out_ref[...] = dot_nn(x_ref[...], k_ref[...]).astype(bf16)

        @pl.when(unit == 2)
        def _():
            out_ref[...] = dot_nn(x_ref[...], v_ref[...]).astype(bf16)

    return pl.pallas_call(
        kernel,
        grid=(3, per),
        in_specs=[
            pl.BlockSpec((width, total), lambda u, c: (0, 0), pipeline_mode=pl.Buffered(1)),
            pl.BlockSpec((dq.shape[0], cols), lambda u, c: (0, jnp.where(u == 0, c, per - 1))),
            pl.BlockSpec((total, cols), lambda u, c: (0, jnp.where(u == 0, 0, jnp.where(u == 1, c, per - 1)))),
            pl.BlockSpec((total, cols), lambda u, c: (0, jnp.where(u == 2, c, 0))),
        ],
        out_specs=pl.BlockSpec((width, cols), lambda u, c: (0, u * per + c)),
        out_shape=jax.ShapeDtypeStruct((width, 3 * width), bf16),
        compiler_params=pltpu.CompilerParams(vmem_limit_bytes=32 * 2**20),
        cost_estimate=pl.CostEstimate(flops=9 * 10**9, bytes_accessed=2 * 10**7, transcendentals=0),
        name="first_gradients",
    )(x_t, dq, dk, dv)


def input_parts(first_grad, dq, dk, dv, w_first):
    seqs, tokens, width = dq.shape
    keys = dk.shape[1]
    pieces = REACH // tokens

    def kernel(first_ref, q_ref, k_ref, v_ref, w_ref, own_ref, rim_ref):
        block = pl.program_id(1)
        part = dot_nt(k_ref[0], w_ref[:, width : 2 * width]) + dot_nt(v_ref[0], w_ref[:, 2 * width :])

        @pl.when(block == pieces)
        def _():
            own_ref[0] = first_ref[0] + part + dot_nt(q_ref[0], w_ref[:, :width])

        @pl.when(block != pieces)
        def _():
            rim_ref[0, 0] = part.astype(bf16)

    own = pl.BlockSpec((1, tokens, width), lambda s, b: (s, 0, 0))
    key = pl.BlockSpec((1, tokens, width), lambda s, b: (s, b, 0))
    return pl.pallas_call(
        kernel,
        grid=(seqs, keys // tokens),
        in_specs=[own, own, key, key,
                  pl.BlockSpec(w_first.shape, lambda s, b: (0, 0), pipeline_mode=pl.Buffered(1))],
        out_specs=[own, pl.BlockSpec((1, 1, tokens, width), lambda s, b: (s, jnp.where(b < pieces, b, jnp.maximum(b - 1, 0)), 0, 0))],
        out_shape=[
            jax.ShapeDtypeStruct((seqs, tokens, width), f32),
            jax.ShapeDtypeStruct((seqs, 2 * pieces, tokens, width), bf16),
        ],
        compiler_params=pltpu.CompilerParams(vmem_limit_bytes=32 * 2**20),
        cost_estimate=pl.CostEstimate(flops=9 * 10**9, bytes_accessed=2 * 10**7, transcendentals=0),
        name="input_parts",
    )(first_grad, dq, dk, dv, w_first)


def on_device(inputs, out_grad, segments, windows, owners, weights, first_moments, second_moments,
              norm_params, norm_first, norm_second):
    seqs, tokens, width = inputs.shape
    rows = seqs * tokens
    heads = windows.shape[0]
    slots = weights.shape[0]
    owner_count = lax.axis_size("seq")
    me = lax.axis_index("seq")
    seq_len = segments.shape[1]
    keys = tokens + 2 * REACH
    pieces = REACH // tokens
    groups = FF // width
    units = owners.shape[0]
    rest = units - 3
    row_count = weights.shape[1]

    ids = jnp.arange(units, dtype=jnp.int32)
    before = (owners[None, :] == owners[:, None]) & (ids[None, :] < ids[:, None])
    rank = jnp.sum(before.astype(jnp.int32), axis=1)
    slot_ids = jnp.arange(owner_count * slots, dtype=jnp.int32)
    match = (owners * slots + rank)[None, :] == slot_ids[:, None]
    unit_of = jnp.max(jnp.where(match, ids[None, :], -1), axis=1)
    my_units = lax.dynamic_slice_in_dim(unit_of, me * slots, slots, 0)

    left = [shifted(inputs, "ctx", pieces - n) for n in range(pieces)]
    right = [shifted(inputs, "ctx", -(n + 1)) for n in range(pieces)]

    low = weights.astype(bf16)
    if owner_count == 2:
        place = jnp.stack([jnp.where(owners == me, 0, 1), rank])
        own_first = pick_units(place[:, :3] * jnp.array([[0], [1]], jnp.int32), [low], 3)
        got_first = swapped(own_first, "seq", 1)
        mine = jnp.repeat(owners[:3] == me, width)[None, :]
        picked_first = jnp.where(mine, own_first, got_first)
        sources = [low, swapped(low, "seq", 1)]
    else:
        every = lax.all_gather(low, "seq", axis=0, tiled=True)
        place = jnp.stack([jnp.zeros_like(owners), owners * slots + rank])
        sources = [every]
        picked_first = pick_units(place[:, :3], sources, 3)
    w_first = lax.all_gather(picked_first, "ctx", axis=0, tiled=True)
    picked_rest = pick_units(place[:, 3:], sources, rest, 1024)
    picked_rest, w_first, left, right = lax.optimization_barrier((picked_rest, w_first, left, right))
    w_rest = lax.all_gather(picked_rest, "ctx", axis=0, tiled=True)

    start = lax.axis_index("ctx") * tokens
    padded = jnp.pad(segments, ((0, 0), (REACH, 0)), constant_values=-1)
    padded = jnp.pad(padded, ((0, 0), (0, REACH)), constant_values=1 << 20)
    key_seg = lax.dynamic_slice_in_dim(padded, start, keys, 1)
    query_seg = key_seg[:, REACH : REACH + tokens]
    lo = jnp.sum((key_seg[:, :, None] < query_seg[:, None, :]).astype(jnp.int32), axis=1)[:, None]
    hi = jnp.sum((key_seg[:, :, None] <= query_seg[:, None, :]).astype(jnp.int32), axis=1)[:, None] - 1
    slopes2 = jnp.power(2.0, -8.0 * (jnp.arange(heads, dtype=f32) + 1.0) / heads) * LOG2E

    x_ext = jnp.concatenate(left + [inputs] + right, axis=1)
    ctx = lax.axis_index("ctx")
    by_core = jnp.transpose(x_ext.reshape(seqs * keys, width)).reshape(width // (2 * row_count), 2, row_count, seqs * keys)
    x_t = jnp.concatenate([lax.dynamic_index_in_dim(by_core, ctx % 2, 1, False), lax.dynamic_index_in_dim(by_core, 1 - ctx % 2, 1, False)])
    x_t = x_t.reshape(width, seqs * keys)
    w_q, w_kv = w_first[:, :width], w_first[:, width:]
    x = inputs.reshape(rows, width)
    q = dot_nn(x, w_q).astype(bf16).reshape(seqs, tokens, width)
    kv = dot_nn(x_ext.reshape(seqs * keys, width), w_kv).astype(bf16).reshape(seqs, keys, 2 * width)
    mixed, lse, peaks = attend_fwd(windows, slopes2, q, kv, lo, hi)
    peak = jnp.max(peaks, axis=(1, 2))
    o = mixed.reshape(rows, width)

    x_t, w_rest = lax.optimization_barrier((x_t, w_rest))
    result, first_grad, o_grad, small, rest_grads = feed_forward(
        o, x, out_grad.reshape(rows, width), w_rest, norm_params
    )
    output = result.reshape(seqs, tokens, width)
    rest_sums = lax.psum_scatter(rest_grads, "ctx", scatter_dimension=0, tiled=True)
    dq, dk, dv = attend_bwd(windows, slopes2, q, kv, o_grad.reshape(seqs, tokens, width), mixed, lo, hi, lse)

    def owned_pair(columns, lowest):
        local = unit_of - lowest
        local = jnp.where((local >= 0) & (local < columns.shape[1] // width), local, -1)
        if owner_count == 2:
            ours = lax.dynamic_slice_in_dim(local, me * slots, slots, 0)
            theirs = lax.dynamic_slice_in_dim(local, (1 - me) * slots, slots, 0)
            return to_slots(ours, columns, slots, width), to_slots(theirs, columns, slots, width)
        return None, to_slots(local, columns, owner_count * slots, width)

    first_grads = first_gradients(
        x_t, dq.reshape(rows, width), dk.reshape(seqs * keys, width), dv.reshape(seqs * keys, width), tokens
    )
    input_grad, rim = input_parts(first_grad.reshape(seqs, tokens, width), dq, dk, dv, w_first)
    half = width // 2
    value = (first_grads[:half].astype(f32) + swapped(first_grads[half:], "ctx", 1).astype(f32)).astype(bf16)
    if owner_count == 2:
        columns = 3 * width // 2
        keep = lax.dynamic_slice_in_dim(value, me * columns, columns, 1)
        got = swapped(lax.dynamic_slice_in_dim(value, (1 - me) * columns, columns, 1), "seq", 1)
        got, input_grad, rim = lax.optimization_barrier((got, input_grad, rim))
        value = (keep.astype(f32) + got.astype(f32)).astype(bf16)
    value = value.reshape(-1, row_count, value.shape[1])

    keep, give = owned_pair(rest_sums, 3)
    bit = 2
    while bit < lax.axis_size("ctx"):
        if 2 * bit == lax.axis_size("ctx"):
            value, give = lax.optimization_barrier((value, give))
        value = halve(value.reshape((-1, 2) + value.shape[1:]), "ctx", bit, 1)
        if bit == 2:
            value, rim = lax.optimization_barrier((value, rim))
        bit *= 2
    first_sums = value[0]
    for n in range(pieces):
        input_grad = input_grad + shifted(rim[:, n], "ctx", n - pieces).astype(f32)
        input_grad = input_grad + shifted(rim[:, pieces + n], "ctx", n + 1).astype(f32)

    is_peak_row = (jnp.arange(8) == 4)[:, None]
    small = jnp.where(is_peak_row, jnp.pad(peak, (0, width - heads))[None], small)
    for axis in ("ctx", "seq"):
        bit = 1
        while bit < lax.axis_size(axis):
            other = swapped(small, axis, bit)
            small = jnp.where(is_peak_row, jnp.maximum(small, other), small + other)
            bit *= 2
    norm_grads = small[:4]
    factors = clip_level / jnp.maximum(small[4, :heads], clip_level)
    column_scale = jnp.repeat(jnp.sqrt(factors), width // heads)[None, :]
    correction = 1.0 - 0.5**STEP

    if owner_count == 2:
        other = swapped(first_sums, "seq", 1)
        whole = jnp.concatenate([jnp.where(me == 0, first_sums, other), jnp.where(me == 0, other, first_sums)], axis=1)
        parts = [keep, swapped(give, "seq", 1), to_slots(jnp.where(my_units < 3, my_units, -1), whole, slots, width)]
    else:
        parts = [lax.psum_scatter(give, "seq", scatter_dimension=0, tiled=True),
                 lax.psum_scatter(owned_pair(first_sums, 0)[1], "seq", scatter_dimension=0, tiled=True)]
    weight_grads, new_weights, new_first, new_second, weights_low = adam_slots(
        my_units, weights, first_moments, second_moments, parts, column_scale, correction, 0.5 / D**0.5
    )
    new_norms, new_norm_first, new_norm_second = adam_step(
        norm_params, norm_grads, norm_first, norm_second, correction, norm_rate
    )
    return (output, input_grad, weight_grads, norm_grads, new_weights, new_first, new_second, weights_low,
            new_norms, new_norm_first, new_norm_second, factors)


def solution(mesh):
    block = P("seq", "ctx", None)
    return jax.shard_map(
        on_device,
        mesh=mesh,
        in_specs=(block, block, P("seq", None), P(), P(), block, block, block, P(), P(), P()),
        out_specs=(block, block, block, P(), block, block, block, block, P(), P(), P(), P()),
        check_vma=False,
    )
```

```python
import jax
import jax.numpy as jnp
from jax import lax
from jax.experimental import pallas as pl
from jax.experimental.pallas import tpu as pltpu
from jax.sharding import PartitionSpec as P

D = 768
FF = 3072
STEP = 3
clip_level = 1.0
decay_rate = 0.1
norm_rate = 0.25
LOG2E = 1.4426950408889634
NEG = -1e30
REACH = 512
QB = 256
bf16 = jnp.bfloat16
f32 = jnp.float32

def dot_nt(a, b):
    return lax.dot_general(a, b, (((1,), (1,)), ((), ())), preferred_element_type=f32)

def dot_nn(a, b):
    return lax.dot_general(a, b, (((1,), (0,)), ((), ())), preferred_element_type=f32)

def fill_bias(bias_ref, slope2):
    rows = bias_ref.shape[0]
    k = lax.broadcasted_iota(jnp.int32, (rows, QB), 0)
    q = lax.broadcasted_iota(jnp.int32, (rows, QB), 1)
    bias_ref[...] = jnp.abs(k - q - REACH).astype(f32) * (-slope2)

def fold8(x, op):
    y = x.reshape(x.shape[0] // 8, 8, x.shape[1])
    return op(y, axis=0)

def head_window(win_ref, lo_ref, hi_ref, head, qb):
    reach = (win_ref[head] - 1) >> 1
    cls = jnp.clip((reach + 127) >> 7, 2, 4)
    qpos = lax.broadcasted_iota(jnp.int32, (1, QB), 1) + (qb * QB + REACH)
    lo = jnp.maximum(lo_ref[0, :, pl.ds(qb * QB, QB)], qpos - reach)
    hi = jnp.minimum(hi_ref[0, :, pl.ds(qb * QB, QB)], qpos + reach)
    return cls, lo, hi

def fwd_kernel(win_ref, slope_ref, q_ref, k_ref, v_ref, lo_ref, hi_ref, o_ref, lse_ref, peak_ref,
               vt_ref, ot_ref, z_ref, bias_ref):
    pair = pl.program_id(0)
    seq = pl.program_id(1)
    tokens = q_ref.shape[1]
    vt_ref[...] = v_ref[0].T

    @pl.when(seq == 0)
    def _():
        peak_ref[...] = jnp.full(peak_ref.shape, NEG, f32)

    rows = lax.broadcasted_iota(jnp.int32, (QB, QB), 0)
    lane = lax.broadcasted_iota(jnp.int32, (1, 128), 1)
    for h in range(2):
        head = pair * 2 + h
        @pl.when(seq == 0)
        def _():
            fill_bias(bias_ref.at[h], slope_ref[head])
        hmask = jnp.where((lane >= h * 64) & (lane < h * 64 + 64), 0.125, 0.0)
        for qb in range(tokens // QB):
            cls, lo, hi = head_window(win_ref, lo_ref, hi_ref, head, qb)
            q = (q_ref[0, pl.ds(qb * QB, QB), :].astype(f32) * hmask).astype(bf16)

            def branch(c):
                reach = c * 128
                first = REACH - reach
                n = 1 + c
                pk = mx = None
                for t in range(n):
                    b = first + t * QB
                    s = dot_nt(k_ref[0, pl.ds(qb * QB + b, QB), :], q)
                    kk = rows + (qb * QB + b)
                    s = jnp.where((kk >= lo) & (kk <= hi), s, NEG)
                    z = s * LOG2E + bias_ref[h, pl.ds(b, QB), :]
                    a, d = fold8(s, jnp.max), fold8(z, jnp.max)
                    pk = a if t == 0 else jnp.maximum(pk, a)
                    mx = d if t == 0 else jnp.maximum(mx, d)
                    z_ref[pl.ds(t * QB, QB), :] = z
                peak_ref[h] = jnp.maximum(peak_ref[h], pk)
                m = jnp.max(mx, axis=0, keepdims=True)
                acc = total = None
                for t in range(n):
                    p = jnp.exp2(z_ref[pl.ds(t * QB, QB), :] - m)
                    e = fold8(p, jnp.sum)
                    total = e if t == 0 else total + e
                    b = first + t * QB
                    part = dot_nn(vt_ref[pl.ds(h * 64, 64), pl.ds(qb * QB + b, QB)], p.astype(bf16))
                    acc = part if t == 0 else acc + part
                total = jnp.sum(total, axis=0, keepdims=True)
                ot_ref[pl.ds(h * 64, 64), pl.ds(qb * QB, QB)] = acc * (1.0 / total)
                lse_ref[0, 0, pl.ds(h, 1), pl.ds(qb * QB, QB)] = m + jnp.log2(total)

            for c in (2, 3, 4):
                pl.when(cls == c)(lambda c=c: branch(c))
    o_ref[0] = ot_ref[...].T.astype(bf16)

def attend_fwd(windows, slopes2, q, kv, lo, hi):
    seqs, tokens, width = q.shape
    keys = kv.shape[1]
    pairs = width // 128
    smem = pl.BlockSpec(memory_space=pltpu.SMEM)
    return pl.pallas_call(
        fwd_kernel,
        grid=(pairs, seqs),
        in_specs=[
            smem, smem,
            pl.BlockSpec((1, tokens, 128), lambda p, s: (s, 0, p)),
            pl.BlockSpec((1, keys, 128), lambda p, s: (s, 0, p)),
            pl.BlockSpec((1, keys, 128), lambda p, s: (s, 0, p + pairs)),
            pl.BlockSpec((1, 1, tokens), lambda p, s: (s, 0, 0)),
            pl.BlockSpec((1, 1, tokens), lambda p, s: (s, 0, 0)),
        ],
        out_specs=[
            pl.BlockSpec((1, tokens, 128), lambda p, s: (s, 0, p)),
            pl.BlockSpec((1, 1, 2, tokens), lambda p, s: (s, p, 0, 0)),
            pl.BlockSpec((2, 8, QB), lambda p, s: (p, 0, 0)),
        ],
        out_shape=[
            jax.ShapeDtypeStruct((seqs, tokens, width), bf16),
            jax.ShapeDtypeStruct((seqs, pairs, 2, tokens), f32),
            jax.ShapeDtypeStruct((2 * pairs, 8, QB), f32),
        ],
        scratch_shapes=[
            pltpu.VMEM((128, keys), bf16),
            pltpu.VMEM((128, tokens), f32),
            pltpu.VMEM((QB + 2 * REACH, QB), f32),
            pltpu.VMEM((2, QB + 2 * REACH, QB), f32),
        ],
        compiler_params=pltpu.CompilerParams(vmem_limit_bytes=40 * 2**20),
        cost_estimate=pl.CostEstimate(flops=2 * 10**10, bytes_accessed=10**7, transcendentals=10**7),
        name="attend_fwd",
    )(windows, slopes2, q, kv, kv, lo, hi)

def bwd_kernel(win_ref, slope_ref, q_ref, k_ref, v_ref, do_ref, o_ref, lo_ref, hi_ref, lse_ref,
               dq_ref, dk_ref, dv_ref, kt_ref, dqt_ref, dka_ref, dva_ref, bias_ref):
    pair = pl.program_id(0)
    seq = pl.program_id(1)
    tokens = q_ref.shape[1]
    kt_ref[...] = k_ref[0].T
    dka_ref[...] = jnp.zeros(dka_ref.shape, f32)
    dva_ref[...] = jnp.zeros(dva_ref.shape, f32)
    lane = lax.broadcasted_iota(jnp.int32, (1, 128), 1)
    ones = jnp.ones((16, 128), bf16)
    for h in range(2):
        head = pair * 2 + h
        @pl.when(seq == 0)
        def _():
            fill_bias(bias_ref.at[h], slope_ref[head])
        inside = (lane >= h * 64) & (lane < h * 64 + 64)
        qmask = jnp.where(inside, 0.125, 0.0)
        dmask = jnp.where(inside, 1.0, 0.0)
        for qb in range(tokens // QB):
            cls, lo, hi = head_window(win_ref, lo_ref, hi_ref, head, qb)
            q = (q_ref[0, pl.ds(qb * QB, QB), :].astype(f32) * qmask).astype(bf16)
            do = (do_ref[0, pl.ds(qb * QB, QB), :].astype(f32) * dmask).astype(bf16)
            lse = lse_ref[0, 0, pl.ds(h, 1), pl.ds(qb * QB, QB)]
            prod = do.astype(f32) * o_ref[0, pl.ds(qb * QB, QB), :].astype(f32)
            prod_hi = prod.astype(bf16)
            prod_lo = (prod - prod_hi.astype(f32)).astype(bf16)
            dsum = (dot_nt(ones, prod_hi) + dot_nt(ones, prod_lo))[:1]

            def branch(c):
                first = REACH - c * 128
                dqt = None
                KB = (1 + c) * QB
                for t in range(1):
                    b = first
                    at = pl.ds(qb * QB + b, KB)
                    s = dot_nt(k_ref[0, at, :], q)
                    dp = dot_nt(v_ref[0, at, :], do)
                    at_first = qb * QB + b
                    rows = lax.broadcasted_iota(jnp.int32, (KB, QB), 0)
                    z = s * LOG2E + (bias_ref[h, pl.ds(b, KB), :] - lse)
                    p = jnp.exp2(jnp.where((rows >= lo - at_first) & (rows <= hi - at_first), z, NEG))
                    ds = (p * (dp - dsum)).astype(bf16)
                    dva_ref[at, :] += dot_nn(p.astype(bf16), do)
                    dka_ref[at, :] += dot_nn(ds, q)
                    part = dot_nn(kt_ref[pl.ds(h * 64, 64), at], ds)
                    dqt = part if t == 0 else dqt + part
                dqt_ref[pl.ds(h * 64, 64), pl.ds(qb * QB, QB)] = dqt * 0.125

            for c in (2, 3, 4):
                pl.when(cls == c)(lambda c=c: branch(c))
    dq_ref[0] = dqt_ref[...].T.astype(bf16)
    dk_ref[0] = dka_ref[...].astype(bf16)
    dv_ref[0] = dva_ref[...].astype(bf16)

def attend_bwd(windows, slopes2, q, kv, do, o, lo, hi, lse):
    seqs, tokens, width = q.shape
    keys = kv.shape[1]
    pairs = width // 128
    smem = pl.BlockSpec(memory_space=pltpu.SMEM)
    tok = pl.BlockSpec((1, tokens, 128), lambda p, s: (s, 0, p))
    key = pl.BlockSpec((1, keys, 128), lambda p, s: (s, 0, p))
    row = pl.BlockSpec((1, 1, tokens), lambda p, s: (s, 0, 0))
    stat = pl.BlockSpec((1, 1, 2, tokens), lambda p, s: (s, p, 0, 0))
    return pl.pallas_call(
        bwd_kernel,
        grid=(pairs, seqs),
        in_specs=[smem, smem, tok, key, pl.BlockSpec((1, keys, 128), lambda p, s: (s, 0, p + pairs)), tok, tok, row, row, stat],
        out_specs=[tok, key, key],
        out_shape=[
            jax.ShapeDtypeStruct((seqs, tokens, width), bf16),
            jax.ShapeDtypeStruct((seqs, keys, width), bf16),
            jax.ShapeDtypeStruct((seqs, keys, width), bf16),
        ],
        scratch_shapes=[
            pltpu.VMEM((128, keys), bf16),
            pltpu.VMEM((128, tokens), f32),
            pltpu.VMEM((keys, 128), f32),
            pltpu.VMEM((keys, 128), f32),
            pltpu.VMEM((2, QB + 2 * REACH, QB), f32),
        ],
        compiler_params=pltpu.CompilerParams(vmem_limit_bytes=40 * 2**20),
        cost_estimate=pl.CostEstimate(flops=5 * 10**10, bytes_accessed=2 * 10**7, transcendentals=10**7),
        name="attend_bwd",
    )(windows, slopes2, q, kv, kv, do, o, lo, hi, lse)

def shifted(value, axis, by):
    peers = lax.axis_size(axis)
    pairs = [(i, i + by) for i in range(peers) if 0 <= i + by < peers]
    return lax.ppermute(value, axis, pairs)


def swapped(value, axis, bit):
    peers = lax.axis_size(axis)
    return lax.ppermute(value, axis, [(i, i ^ bit) for i in range(peers)])


def layer_norm(rows_in):
    center = rows_in - jnp.mean(rows_in, axis=-1, keepdims=True)
    spread = jnp.mean(center * center, axis=-1, keepdims=True)
    scale = lax.rsqrt(spread + 1e-05)
    return center * scale, scale


def layer_norm_back(grad, hat, scale, gain):
    inner = grad * gain
    mean_one = jnp.mean(inner, axis=-1, keepdims=True)
    mean_two = jnp.mean(inner * hat, axis=-1, keepdims=True)
    back = scale * (inner - mean_one - hat * mean_two)
    return back, jnp.sum(grad * hat, axis=0, keepdims=True), jnp.sum(grad, axis=0, keepdims=True)


def exchange(small, keep, give, axis, bit, beside=()):
    high = small.astype(bf16)
    both = jnp.concatenate([high, (small - high.astype(f32)).astype(bf16)])
    lead, cols = give.shape[:-2], give.shape[-1]
    flat = give.reshape(-1, cols)
    tail = jnp.pad(both, ((0, 0), (0, cols - both.shape[1])))
    got = swapped(jnp.concatenate([flat, tail]), axis, bit)
    if beside:
        got, beside = lax.optimization_barrier((got, beside))
    terms = got[flat.shape[0] :, : both.shape[1]].astype(f32)
    theirs = terms[:8] + terms[8:]
    ours = both[:8].astype(f32) + both[8:].astype(f32)
    is_peak_row = lax.broadcasted_iota(jnp.int32, (8, 1), 0) == 4
    small = jnp.where(is_peak_row, jnp.maximum(ours, theirs), ours + theirs)
    total = (keep.astype(f32) + got[: flat.shape[0]].reshape(give.shape).astype(f32)).astype(bf16)
    return (small, total, *beside)


def halve(small, value, axis, bit):
    side = (lax.axis_index(axis) // bit) % 2
    keep = lax.dynamic_index_in_dim(value, side, 1, False)
    return exchange(small, keep, lax.dynamic_index_in_dim(value, 1 - side, 1, False), axis, bit)


def pick_units(slot_of, sources, count, pad=0):
    slots, rows, width = sources[0].shape

    def kernel(slot_ref, *refs):
        out_ref = refs[-1]
        if pad:
            out_ref[:, pl.ds(count * width, pad)] = jnp.zeros((rows, pad), out_ref.dtype)
        for u in range(count):
            at = pl.ds(u * width, width)
            for number, ref in enumerate(refs[:-1]):

                @pl.when(slot_ref[0, u] == number)
                def _(ref=ref, u=u, at=at):
                    out_ref[:, at] = ref[slot_ref[1, u]]

    vmem = pl.BlockSpec(memory_space=pltpu.VMEM)
    return pl.pallas_call(
        kernel,
        in_specs=[pl.BlockSpec(memory_space=pltpu.SMEM)] + [vmem] * len(sources),
        out_specs=vmem,
        out_shape=jax.ShapeDtypeStruct((rows, count * width + pad), sources[0].dtype),
        compiler_params=pltpu.CompilerParams(vmem_limit_bytes=24 * 2**20),
        name="pick_units",
    )(slot_of, *sources)


def to_slots(unit_of, columns, slots, width):
    rows = columns.shape[0]

    def kernel(unit_ref, col_ref, out_ref):
        for s in range(slots):
            unit = unit_ref[s]

            @pl.when(unit >= 0)
            def _(s=s, unit=unit):
                out_ref[s] = col_ref[:, pl.ds(pl.multiple_of(unit * width, 128), width)]

            @pl.when(unit < 0)
            def _(s=s):
                out_ref[s] = jnp.zeros((rows, width), out_ref.dtype)

    vmem = pl.BlockSpec(memory_space=pltpu.VMEM)
    return pl.pallas_call(
        kernel,
        in_specs=[pl.BlockSpec(memory_space=pltpu.SMEM), vmem],
        out_specs=vmem,
        out_shape=jax.ShapeDtypeStruct((slots, rows, width), columns.dtype),
        compiler_params=pltpu.CompilerParams(vmem_limit_bytes=24 * 2**20),
        name="to_slots",
    )(unit_of, columns)


def adam_slots(unit_of, weights, first, second, grads, scale, correction, rate):
    slots, rows, width = weights.shape

    def kernel(unit_ref, w_ref, m_ref, v_ref, scale_ref, *refs):
        grad_refs, (g_out, w_out, m_out, v_out, low_out) = refs[:-5], refs[-5:]
        unit = unit_ref[pl.program_id(0)]
        live = unit >= 0
        g = grad_refs[0][0].astype(f32)
        for ref in grad_refs[1:]:
            g = g + ref[0].astype(f32)
        g = jnp.where(live, g, 0.0)
        w = w_ref[0]
        m = 0.5 * m_ref[0] + 0.5 * g
        v = 0.5 * v_ref[0] + 0.5 * g * g
        step = m * (1.0 / correction) / (jnp.sqrt(v * (1.0 / correction)) + 1e-08)
        moved = w - rate * (step + decay_rate * w)
        moved = jnp.where((unit == 0) | (unit == 1), moved * scale_ref[...], moved)
        moved = jnp.where(live, moved, 0.0)
        g_out[0] = g
        w_out[0] = moved
        m_out[0] = jnp.where(live, m, 0.0)
        v_out[0] = jnp.where(live, v, 0.0)
        low_out[0] = moved.astype(bf16)

    block = pl.BlockSpec((1, rows, width), lambda s: (s, 0, 0))
    wide = jax.ShapeDtypeStruct(weights.shape, f32)
    return pl.pallas_call(
        kernel,
        grid=(slots,),
        in_specs=[pl.BlockSpec(memory_space=pltpu.SMEM), block, block, block,
                  pl.BlockSpec((1, width), lambda s: (0, 0))] + [block] * len(grads),
        out_specs=[block] * 5,
        out_shape=[wide] * 4 + [jax.ShapeDtypeStruct(weights.shape, bf16)],
        compiler_params=pltpu.CompilerParams(vmem_limit_bytes=24 * 2**20),
        name="adam_slots",
    )(unit_of, weights, first, second, scale, *grads)


def adam_step(master, gradient, first, second, correction, learn_rate):
    new_first = 0.5 * first + 0.5 * gradient
    new_second = 0.5 * second + 0.5 * gradient * gradient
    normed = new_first / correction / (jnp.sqrt(new_second / correction) + 1e-08)
    return (master - learn_rate * (normed + decay_rate * master), new_first, new_second)


def dot_tn(a, b):
    return lax.dot_general(a, b, (((0,), (0,)), ((), ())), preferred_element_type=f32)


def gelu_parts(gate):
    cdf = 0.5 * (1.0 + lax.erf(gate * 0.7071067811865476))
    density = 0.3989422804014327 * jnp.exp(-0.5 * gate * gate)
    return cdf, density


RB = 512
CHUNK = 256


def ffn_kernel(o_ref, x_ref, og_ref, wo_ref, wg_ref, wu_ref, wd_ref, norm_ref,
               out_ref, first_ref, ograd_ref, small_ref, grads_ref,
               hat_ref, scale_ref, acc_ref, a_ref, b_ref, h_ref, ylow_ref, ylowt_ref, fgrad_ref,
               gg_ref, ug_ref, stage_g, stage_u, stage_d, stage_o, sems):
    step = pl.program_id(0)
    rows, width = x_ref.shape
    chunk = wg_ref.shape[1]
    chunks = FF // chunk
    blocks = rows // RB

    def at(i):
        return pl.ds(i * RB, RB)

    def copies(j):
        slot = lax.rem(j, 2)
        column = pl.multiple_of(width + j * chunk, 128)
        per = width // chunk
        return (
            pltpu.make_async_copy(stage_g.at[slot], grads_ref.at[:, pl.ds(column, chunk)], sems.at[slot, 0]),
            pltpu.make_async_copy(stage_u.at[slot], grads_ref.at[:, pl.ds(column + FF, chunk)], sems.at[slot, 1]),
            pltpu.make_async_copy(
                stage_d.at[slot],
                grads_ref.at[pl.ds(pl.multiple_of(lax.rem(j, per) * chunk, 128), chunk),
                             pl.ds(pl.multiple_of(width + 2 * FF + lax.div(j, per) * width, 128), width)],
                sems.at[slot, 2],
            ),
        )

    @pl.when(step == 0)
    def _():
        for i in range(blocks):
            total = x_ref[at(i), :].astype(f32) + dot_nn(o_ref[at(i), :], wo_ref[...])
            hat, scale = layer_norm(total)
            y1 = hat * norm_ref[0:1, :] + norm_ref[1:2, :]
            hat_ref[at(i), :] = hat
            scale_ref[at(i), :] = scale
            acc_ref[at(i), :] = y1
            ylow_ref[at(i), :] = y1.astype(bf16)
            ylowt_ref[:, at(i)] = y1.T.astype(bf16)

    @pl.when(step < chunks)
    def _():
        for i in range(blocks):
            y = ylow_ref[at(i), :]
            gate = dot_nn(y, wg_ref[...])
            up = dot_nn(y, wu_ref[...])
            cdf, density = gelu_parts(gate)
            a = gate * cdf
            hidden = (a * up).astype(bf16)
            a_ref[step, at(i), :] = a.astype(bf16)
            b_ref[step, at(i), :] = (up * (cdf + gate * density)).astype(bf16)
            h_ref[step, at(i), :] = hidden
            acc_ref[at(i), :] += dot_nn(hidden, wd_ref[...])

    @pl.when(step == chunks)
    def _():
        gain = bias = None
        for i in range(blocks):
            hat, scale = layer_norm(acc_ref[at(i), :])
            out_ref[at(i), :] = (hat * norm_ref[2:3, :] + norm_ref[3:4, :]).astype(bf16)
            grad = og_ref[at(i), :].astype(f32)
            back, g, b = layer_norm_back(grad, hat, scale, norm_ref[2:3, :])
            gain = g if i == 0 else gain + g
            bias = b if i == 0 else bias + b
            acc_ref[at(i), :] = back
            fgrad_ref[at(i), :] = back.astype(bf16)
        small_ref[2:3, :] = gain
        small_ref[3:4, :] = bias

    @pl.when(step >= chunks)
    def _():
        j = step - chunks
        slot = lax.rem(j, 2)

        @pl.when(j >= 2)
        def _():
            for copy in copies(j - 2):
                copy.wait()

        for i in range(blocks):
            hidden_grad = dot_nt(fgrad_ref[at(i), :], wd_ref[...])
            gg = (hidden_grad * b_ref[j, at(i), :].astype(f32)).astype(bf16)
            ug = (hidden_grad * a_ref[j, at(i), :].astype(f32)).astype(bf16)
            gg_ref[at(i), :] = gg
            ug_ref[at(i), :] = ug
            acc_ref[at(i), :] += dot_nt(gg, wg_ref[...]) + dot_nt(ug, wu_ref[...])
        stage_g[slot] = dot_nn(ylowt_ref[...], gg_ref[...]).astype(bf16)
        stage_u[slot] = dot_nn(ylowt_ref[...], ug_ref[...]).astype(bf16)
        stage_d[slot] = dot_tn(h_ref[j], fgrad_ref[...]).astype(bf16)
        for copy in copies(j):
            copy.start()

    @pl.when(step == 2 * chunks - 1)
    def _():
        gain = bias = None
        for i in range(blocks):
            back, g, b = layer_norm_back(acc_ref[at(i), :], hat_ref[at(i), :], scale_ref[at(i), :], norm_ref[0:1, :])
            gain = g if i == 0 else gain + g
            bias = b if i == 0 else bias + b
            first_ref[at(i), :] = back
            low = back.astype(bf16)
            fgrad_ref[at(i), :] = low
            ograd_ref[at(i), :] = dot_nt(low, wo_ref[...]).astype(bf16)
        small_ref[0:1, :] = gain
        small_ref[1:2, :] = bias
        small_ref[4:8, :] = jnp.zeros((4, width), f32)
        stage_o[...] = dot_tn(o_ref[...], fgrad_ref[...]).astype(bf16)
        last = pltpu.make_async_copy(stage_o, grads_ref.at[:, pl.ds(0, width)], sems.at[2, 0])
        last.start()
        for j in (chunks - 2, chunks - 1):
            for copy in copies(j):
                copy.wait()
        last.wait()


def feed_forward(o, x, out_grad, w_rest, norms):
    rows, width = x.shape
    chunks = FF // CHUNK
    lead = width // CHUNK
    per = width // CHUNK

    def whole(shape):
        return pl.BlockSpec(shape, lambda s: (0,) * len(shape), pipeline_mode=pl.Buffered(1))

    full = whole((rows, width))
    return pl.pallas_call(
        ffn_kernel,
        grid=(2 * chunks,),
        in_specs=[
            full, full, full,
            whole((width, width)),
            pl.BlockSpec((width, CHUNK), lambda s: (0, lead + lax.rem(s, chunks))),
            pl.BlockSpec((width, CHUNK), lambda s: (0, lead + chunks + lax.rem(s, chunks))),
            pl.BlockSpec((CHUNK, width), lambda s: (lax.rem(lax.rem(s, chunks), per), 1 + 2 * FF // width + lax.div(lax.rem(s, chunks), per))),
            whole(norms.shape),
        ],
        out_specs=[full, full, full, whole((8, width)), pl.BlockSpec(memory_space=pl.ANY)],
        out_shape=[
            jax.ShapeDtypeStruct((rows, width), bf16),
            jax.ShapeDtypeStruct((rows, width), f32),
            jax.ShapeDtypeStruct((rows, width), bf16),
            jax.ShapeDtypeStruct((8, width), f32),
            jax.ShapeDtypeStruct((width, width + 3 * FF), bf16),
        ],
        scratch_shapes=[
            pltpu.VMEM((rows, width), f32),
            pltpu.VMEM((rows, 1), f32),
            pltpu.VMEM((rows, width), f32),
            pltpu.VMEM((chunks, rows, CHUNK), bf16),
            pltpu.VMEM((chunks, rows, CHUNK), bf16),
            pltpu.VMEM((chunks, rows, CHUNK), bf16),
            pltpu.VMEM((rows, width), bf16),
            pltpu.VMEM((width, rows), bf16),
            pltpu.VMEM((rows, width), bf16),
            pltpu.VMEM((rows, CHUNK), bf16),
            pltpu.VMEM((rows, CHUNK), bf16),
            pltpu.VMEM((2, width, CHUNK), bf16),
            pltpu.VMEM((2, width, CHUNK), bf16),
            pltpu.VMEM((2, CHUNK, width), bf16),
            pltpu.VMEM((width, width), bf16),
            pltpu.SemaphoreType.DMA((3, 3)),
        ],
        compiler_params=pltpu.CompilerParams(vmem_limit_bytes=58 * 2**20),
        cost_estimate=pl.CostEstimate(flops=46 * 10**9, bytes_accessed=6 * 10**7, transcendentals=6 * 10**6),
        name="feed_forward",
    )(o, x, out_grad, w_rest, w_rest, w_rest, w_rest, norms)

def first_gradients(x_t, dq, dk, dv, tokens):
    width, total = x_t.shape
    seqs = dq.shape[0] // tokens
    keys = total // seqs
    cols = 256
    per = width // cols

    def kernel(x_ref, q_ref, k_ref, v_ref, out_ref):
        unit = pl.program_id(0)

        @pl.when(unit == 0)
        def _():
            acc = None
            for s in range(seqs):
                part = dot_nn(x_ref[:, pl.ds(s * keys + REACH, tokens)], q_ref[pl.ds(s * tokens, tokens), :])
                acc = part if s == 0 else acc + part
            out_ref[...] = acc.astype(bf16)

        @pl.when(unit == 1)
        def _():
            out_ref[...] = dot_nn(x_ref[...], k_ref[...]).astype(bf16)

        @pl.when(unit == 2)
        def _():
            out_ref[...] = dot_nn(x_ref[...], v_ref[...]).astype(bf16)

    return pl.pallas_call(
        kernel,
        grid=(3, per),
        in_specs=[
            pl.BlockSpec((width, total), lambda u, c: (0, 0), pipeline_mode=pl.Buffered(1)),
            pl.BlockSpec((dq.shape[0], cols), lambda u, c: (0, jnp.where(u == 0, c, per - 1))),
            pl.BlockSpec((total, cols), lambda u, c: (0, jnp.where(u == 0, 0, jnp.where(u == 1, c, per - 1)))),
            pl.BlockSpec((total, cols), lambda u, c: (0, jnp.where(u == 2, c, 0))),
        ],
        out_specs=pl.BlockSpec((width, cols), lambda u, c: (0, u * per + c)),
        out_shape=jax.ShapeDtypeStruct((width, 3 * width), bf16),
        compiler_params=pltpu.CompilerParams(vmem_limit_bytes=32 * 2**20),
        cost_estimate=pl.CostEstimate(flops=9 * 10**9, bytes_accessed=2 * 10**7, transcendentals=0),
        name="first_gradients",
    )(x_t, dq, dk, dv)


def input_parts(first_grad, dq, dk, dv, w_first):
    seqs, tokens, width = dq.shape
    keys = dk.shape[1]
    pieces = REACH // tokens

    def kernel(first_ref, q_ref, k_ref, v_ref, w_ref, own_ref, rim_ref):
        block = pl.program_id(1)
        part = dot_nt(k_ref[0], w_ref[:, width : 2 * width]) + dot_nt(v_ref[0], w_ref[:, 2 * width :])

        @pl.when(block == pieces)
        def _():
            own_ref[0] = first_ref[0] + part + dot_nt(q_ref[0], w_ref[:, :width])

        @pl.when(block != pieces)
        def _():
            rim_ref[0, 0] = part.astype(bf16)

    own = pl.BlockSpec((1, tokens, width), lambda s, b: (s, 0, 0))
    key = pl.BlockSpec((1, tokens, width), lambda s, b: (s, b, 0))
    return pl.pallas_call(
        kernel,
        grid=(seqs, keys // tokens),
        in_specs=[own, own, key, key,
                  pl.BlockSpec(w_first.shape, lambda s, b: (0, 0), pipeline_mode=pl.Buffered(1))],
        out_specs=[own, pl.BlockSpec((1, 1, tokens, width), lambda s, b: (s, jnp.where(b < pieces, b, jnp.maximum(b - 1, 0)), 0, 0))],
        out_shape=[
            jax.ShapeDtypeStruct((seqs, tokens, width), f32),
            jax.ShapeDtypeStruct((seqs, 2 * pieces, tokens, width), bf16),
        ],
        compiler_params=pltpu.CompilerParams(vmem_limit_bytes=32 * 2**20),
        cost_estimate=pl.CostEstimate(flops=9 * 10**9, bytes_accessed=2 * 10**7, transcendentals=0),
        name="input_parts",
    )(first_grad, dq, dk, dv, w_first)


def on_device(inputs, out_grad, segments, windows, owners, weights, first_moments, second_moments,
              norm_params, norm_first, norm_second):
    seqs, tokens, width = inputs.shape
    rows = seqs * tokens
    heads = windows.shape[0]
    slots = weights.shape[0]
    owner_count = lax.axis_size("seq")
    me = lax.axis_index("seq")
    seq_len = segments.shape[1]
    keys = tokens + 2 * REACH
    pieces = REACH // tokens
    groups = FF // width
    units = owners.shape[0]
    rest = units - 3
    row_count = weights.shape[1]

    ids = jnp.arange(units, dtype=jnp.int32)
    before = (owners[None, :] == owners[:, None]) & (ids[None, :] < ids[:, None])
    rank = jnp.sum(before.astype(jnp.int32), axis=1)
    slot_ids = jnp.arange(owner_count * slots, dtype=jnp.int32)
    match = (owners * slots + rank)[None, :] == slot_ids[:, None]
    unit_of = jnp.max(jnp.where(match, ids[None, :], -1), axis=1)
    my_units = lax.dynamic_slice_in_dim(unit_of, me * slots, slots, 0)

    left = [shifted(inputs, "ctx", pieces - n) for n in range(pieces)]
    right = [shifted(inputs, "ctx", -(n + 1)) for n in range(pieces)]

    low = weights.astype(bf16)
    if owner_count == 2:
        place = jnp.stack([jnp.where(owners == me, 0, 1), rank])
        own_first = pick_units(place[:, :3] * jnp.array([[0], [1]], jnp.int32), [low], 3)
        got_first = swapped(own_first, "seq", 1)
        mine = jnp.repeat(owners[:3] == me, width)[None, :]
        picked_first = jnp.where(mine, own_first, got_first)
        sources = [low, swapped(low, "seq", 1)]
    else:
        every = lax.all_gather(low, "seq", axis=0, tiled=True)
        place = jnp.stack([jnp.zeros_like(owners), owners * slots + rank])
        sources = [every]
        picked_first = pick_units(place[:, :3], sources, 3)
    w_first = lax.all_gather(picked_first, "ctx", axis=0, tiled=True)
    picked_rest = pick_units(place[:, 3:], sources, rest, 1024)
    picked_rest, w_first, left, right = lax.optimization_barrier((picked_rest, w_first, left, right))
    w_rest = lax.all_gather(picked_rest, "ctx", axis=0, tiled=True)

    start = lax.axis_index("ctx") * tokens
    padded = jnp.pad(segments, ((0, 0), (REACH, 0)), constant_values=-1)
    padded = jnp.pad(padded, ((0, 0), (0, REACH)), constant_values=1 << 20)
    key_seg = lax.dynamic_slice_in_dim(padded, start, keys, 1)
    query_seg = key_seg[:, REACH : REACH + tokens]
    lo = jnp.sum((key_seg[:, :, None] < query_seg[:, None, :]).astype(jnp.int32), axis=1)[:, None]
    hi = jnp.sum((key_seg[:, :, None] <= query_seg[:, None, :]).astype(jnp.int32), axis=1)[:, None] - 1
    slopes2 = jnp.power(2.0, -8.0 * (jnp.arange(heads, dtype=f32) + 1.0) / heads) * LOG2E

    x_ext = jnp.concatenate(left + [inputs] + right, axis=1)
    ctx = lax.axis_index("ctx")
    by_core = jnp.transpose(x_ext.reshape(seqs * keys, width)).reshape(width // (2 * row_count), 2, row_count, seqs * keys)
    x_t = jnp.concatenate([lax.dynamic_index_in_dim(by_core, ctx % 2, 1, False), lax.dynamic_index_in_dim(by_core, 1 - ctx % 2, 1, False)])
    x_t = x_t.reshape(width, seqs * keys)
    w_q, w_kv = w_first[:, :width], w_first[:, width:]
    x = inputs.reshape(rows, width)
    q = dot_nn(x, w_q).astype(bf16).reshape(seqs, tokens, width)
    kv = dot_nn(x_ext.reshape(seqs * keys, width), w_kv).astype(bf16).reshape(seqs, keys, 2 * width)
    mixed, lse, peaks = attend_fwd(windows, slopes2, q, kv, lo, hi)
    peak = jnp.max(peaks, axis=(1, 2))
    o = mixed.reshape(rows, width)

    x_t, w_rest = lax.optimization_barrier((x_t, w_rest))
    result, first_grad, o_grad, small, rest_grads = feed_forward(
        o, x, out_grad.reshape(rows, width), w_rest, norm_params
    )
    output = result.reshape(seqs, tokens, width)
    rest_sums = lax.psum_scatter(rest_grads, "ctx", scatter_dimension=0, tiled=True)
    dq, dk, dv = attend_bwd(windows, slopes2, q, kv, o_grad.reshape(seqs, tokens, width), mixed, lo, hi, lse)

    def owned_pair(columns, lowest):
        local = unit_of - lowest
        local = jnp.where((local >= 0) & (local < columns.shape[1] // width), local, -1)
        if owner_count == 2:
            ours = lax.dynamic_slice_in_dim(local, me * slots, slots, 0)
            theirs = lax.dynamic_slice_in_dim(local, (1 - me) * slots, slots, 0)
            return to_slots(ours, columns, slots, width), to_slots(theirs, columns, slots, width)
        return None, to_slots(local, columns, owner_count * slots, width)

    input_grad, rim = input_parts(first_grad.reshape(seqs, tokens, width), dq, dk, dv, w_first)

    is_peak_row = (jnp.arange(8) == 4)[:, None]
    small = jnp.where(is_peak_row, jnp.pad(peak, (0, width - heads))[None], small)
    first_grads = first_gradients(
        x_t, dq.reshape(rows, width), dk.reshape(seqs * keys, width), dv.reshape(seqs * keys, width), tokens
    )
    half = width // 2
    small, value = exchange(small, first_grads[:half], first_grads[half:], "ctx", 1)
    if owner_count == 2:
        columns = 3 * width // 2
        small, value, input_grad, rim = exchange(
            small,
            lax.dynamic_slice_in_dim(value, me * columns, columns, 1),
            lax.dynamic_slice_in_dim(value, (1 - me) * columns, columns, 1),
            "seq", 1, (input_grad, rim),
        )
    value = value.reshape(-1, row_count, value.shape[1])
    keep, give = owned_pair(rest_sums, 3)
    bit = 2
    arrived = []
    while bit < lax.axis_size("ctx"):
        if 2 * bit == lax.axis_size("ctx"):
            value, arrived, _ = lax.optimization_barrier((value, arrived, give))
        small, value = halve(small, value.reshape((-1, 2) + value.shape[1:]), "ctx", bit)
        if bit == 2:
            for n in range(pieces):
                arrived += [shifted(rim[:, n], "ctx", n - pieces), shifted(rim[:, pieces + n], "ctx", n + 1)]
        bit *= 2
    for piece in arrived:
        input_grad = input_grad + piece.astype(f32)
    first_sums = value[0]
    bit = 1
    while owner_count != 2 and bit < owner_count:
        other = swapped(small, "seq", bit)
        small = jnp.where(is_peak_row, jnp.maximum(small, other), small + other)
        bit *= 2
    norm_grads = small[:4]
    factors = clip_level / jnp.maximum(small[4, :heads], clip_level)
    column_scale = jnp.repeat(jnp.sqrt(factors), width // heads)[None, :]
    correction = 1.0 - 0.5**STEP

    if owner_count == 2:
        other = swapped(first_sums, "seq", 1)
        whole = jnp.concatenate([jnp.where(me == 0, first_sums, other), jnp.where(me == 0, other, first_sums)], axis=1)
        parts = [keep, swapped(give, "seq", 1), to_slots(jnp.where(my_units < 3, my_units, -1), whole, slots, width)]
    else:
        parts = [lax.psum_scatter(give, "seq", scatter_dimension=0, tiled=True),
                 lax.psum_scatter(owned_pair(first_sums, 0)[1], "seq", scatter_dimension=0, tiled=True)]
    weight_grads, new_weights, new_first, new_second, weights_low = adam_slots(
        my_units, weights, first_moments, second_moments, parts, column_scale, correction, 0.5 / D**0.5
    )
    new_norms, new_norm_first, new_norm_second = adam_step(
        norm_params, norm_grads, norm_first, norm_second, correction, norm_rate
    )
    return (output, input_grad, weight_grads, norm_grads, new_weights, new_first, new_second, weights_low,
            new_norms, new_norm_first, new_norm_second, factors)


def solution(mesh):
    block = P("seq", "ctx", None)
    return jax.shard_map(
        on_device,
        mesh=mesh,
        in_specs=(block, block, P("seq", None), P(), P(), block, block, block, P(), P(), P()),
        out_specs=(block, block, block, P(), block, block, block, block, P(), P(), P(), P()),
        check_vma=False,
    )
```

```python
import jax
import jax.numpy as jnp
from jax import lax
from jax.experimental import pallas as pl
from jax.experimental.pallas import tpu as pltpu
from jax.sharding import PartitionSpec as P

D = 768
FF = 3072
STEP = 3
clip_level = 1.0
decay_rate = 0.1
norm_rate = 0.25
LOG2E = 1.4426950408889634
NEG = -1e30
REACH = 512
QB = 256
bf16 = jnp.bfloat16
f32 = jnp.float32

def dot_nt(a, b):
    return lax.dot_general(a, b, (((1,), (1,)), ((), ())), preferred_element_type=f32)

def dot_nn(a, b):
    return lax.dot_general(a, b, (((1,), (0,)), ((), ())), preferred_element_type=f32)

def fill_bias(bias_ref, slope2):
    rows = bias_ref.shape[0]
    k = lax.broadcasted_iota(jnp.int32, (rows, QB), 0)
    q = lax.broadcasted_iota(jnp.int32, (rows, QB), 1)
    bias_ref[...] = jnp.abs(k - q - REACH).astype(f32) * (-slope2)

def fold8(x, op):
    y = x.reshape(x.shape[0] // 8, 8, x.shape[1])
    return op(y, axis=0)

def head_window(win_ref, lo_ref, hi_ref, head, qb):
    reach = (win_ref[head] - 1) >> 1
    cls = jnp.clip((reach + 127) >> 7, 2, 4)
    qpos = lax.broadcasted_iota(jnp.int32, (1, QB), 1) + (qb * QB + REACH)
    lo = jnp.maximum(lo_ref[0, :, pl.ds(qb * QB, QB)], qpos - reach)
    hi = jnp.minimum(hi_ref[0, :, pl.ds(qb * QB, QB)], qpos + reach)
    return cls, lo, hi

def fwd_kernel(win_ref, slope_ref, q_ref, k_ref, v_ref, lo_ref, hi_ref, o_ref, lse_ref, peak_ref,
               vt_ref, ot_ref, z_ref, bias_ref):
    pair = pl.program_id(0)
    seq = pl.program_id(1)
    tokens = q_ref.shape[1]
    vt_ref[...] = v_ref[0].T

    @pl.when(seq == 0)
    def _():
        peak_ref[...] = jnp.full(peak_ref.shape, NEG, f32)

    rows = lax.broadcasted_iota(jnp.int32, (QB, QB), 0)
    lane = lax.broadcasted_iota(jnp.int32, (1, 128), 1)
    for h in range(2):
        head = pair * 2 + h
        @pl.when(seq == 0)
        def _():
            fill_bias(bias_ref.at[h], slope_ref[head])
        hmask = jnp.where((lane >= h * 64) & (lane < h * 64 + 64), 0.125, 0.0)
        for qb in range(tokens // QB):
            cls, lo, hi = head_window(win_ref, lo_ref, hi_ref, head, qb)
            q = (q_ref[0, pl.ds(qb * QB, QB), :].astype(f32) * hmask).astype(bf16)

            def branch(c):
                reach = c * 128
                first = REACH - reach
                n = 1 + c
                pk = mx = None
                for t in range(n):
                    b = first + t * QB
                    s = dot_nt(k_ref[0, pl.ds(qb * QB + b, QB), :], q)
                    kk = rows + (qb * QB + b)
                    s = jnp.where((kk >= lo) & (kk <= hi), s, NEG)
                    z = s * LOG2E + bias_ref[h, pl.ds(b, QB), :]
                    a, d = fold8(s, jnp.max), fold8(z, jnp.max)
                    pk = a if t == 0 else jnp.maximum(pk, a)
                    mx = d if t == 0 else jnp.maximum(mx, d)
                    z_ref[pl.ds(t * QB, QB), :] = z
                peak_ref[h] = jnp.maximum(peak_ref[h], pk)
                m = jnp.max(mx, axis=0, keepdims=True)
                acc = total = None
                for t in range(n):
                    p = jnp.exp2(z_ref[pl.ds(t * QB, QB), :] - m)
                    e = fold8(p, jnp.sum)
                    total = e if t == 0 else total + e
                    b = first + t * QB
                    part = dot_nn(vt_ref[pl.ds(h * 64, 64), pl.ds(qb * QB + b, QB)], p.astype(bf16))
                    acc = part if t == 0 else acc + part
                total = jnp.sum(total, axis=0, keepdims=True)
                ot_ref[pl.ds(h * 64, 64), pl.ds(qb * QB, QB)] = acc * (1.0 / total)
                lse_ref[0, 0, pl.ds(h, 1), pl.ds(qb * QB, QB)] = m + jnp.log2(total)

            for c in (2, 3, 4):
                pl.when(cls == c)(lambda c=c: branch(c))
    o_ref[0] = ot_ref[...].T.astype(bf16)

def attend_fwd(windows, slopes2, q, kv, lo, hi):
    seqs, tokens, width = q.shape
    keys = kv.shape[1]
    pairs = width // 128
    smem = pl.BlockSpec(memory_space=pltpu.SMEM)
    return pl.pallas_call(
        fwd_kernel,
        grid=(pairs, seqs),
        in_specs=[
            smem, smem,
            pl.BlockSpec((1, tokens, 128), lambda p, s: (s, 0, p)),
            pl.BlockSpec((1, keys, 128), lambda p, s: (s, 0, p)),
            pl.BlockSpec((1, keys, 128), lambda p, s: (s, 0, p + pairs)),
            pl.BlockSpec((1, 1, tokens), lambda p, s: (s, 0, 0)),
            pl.BlockSpec((1, 1, tokens), lambda p, s: (s, 0, 0)),
        ],
        out_specs=[
            pl.BlockSpec((1, tokens, 128), lambda p, s: (s, 0, p)),
            pl.BlockSpec((1, 1, 2, tokens), lambda p, s: (s, p, 0, 0)),
            pl.BlockSpec((2, 8, QB), lambda p, s: (p, 0, 0)),
        ],
        out_shape=[
            jax.ShapeDtypeStruct((seqs, tokens, width), bf16),
            jax.ShapeDtypeStruct((seqs, pairs, 2, tokens), f32),
            jax.ShapeDtypeStruct((2 * pairs, 8, QB), f32),
        ],
        scratch_shapes=[
            pltpu.VMEM((128, keys), bf16),
            pltpu.VMEM((128, tokens), f32),
            pltpu.VMEM((QB + 2 * REACH, QB), f32),
            pltpu.VMEM((2, QB + 2 * REACH, QB), f32),
        ],
        compiler_params=pltpu.CompilerParams(vmem_limit_bytes=40 * 2**20),
        cost_estimate=pl.CostEstimate(flops=2 * 10**10, bytes_accessed=10**7, transcendentals=10**7),
        name="attend_fwd",
    )(windows, slopes2, q, kv, kv, lo, hi)

def bwd_kernel(win_ref, slope_ref, q_ref, k_ref, v_ref, do_ref, o_ref, lo_ref, hi_ref, lse_ref,
               dq_ref, dk_ref, dv_ref, kt_ref, dqt_ref, dka_ref, dva_ref, bias_ref):
    pair = pl.program_id(0)
    seq = pl.program_id(1)
    tokens = q_ref.shape[1]
    kt_ref[...] = k_ref[0].T
    dka_ref[...] = jnp.zeros(dka_ref.shape, f32)
    dva_ref[...] = jnp.zeros(dva_ref.shape, f32)
    lane = lax.broadcasted_iota(jnp.int32, (1, 128), 1)
    ones = jnp.ones((16, 128), bf16)
    for h in range(2):
        head = pair * 2 + h
        @pl.when(seq == 0)
        def _():
            fill_bias(bias_ref.at[h], slope_ref[head])
        inside = (lane >= h * 64) & (lane < h * 64 + 64)
        qmask = jnp.where(inside, 0.125, 0.0)
        dmask = jnp.where(inside, 1.0, 0.0)
        for qb in range(tokens // QB):
            cls, lo, hi = head_window(win_ref, lo_ref, hi_ref, head, qb)
            q = (q_ref[0, pl.ds(qb * QB, QB), :].astype(f32) * qmask).astype(bf16)
            do = (do_ref[0, pl.ds(qb * QB, QB), :].astype(f32) * dmask).astype(bf16)
            lse = lse_ref[0, 0, pl.ds(h, 1), pl.ds(qb * QB, QB)]
            prod = do.astype(f32) * o_ref[0, pl.ds(qb * QB, QB), :].astype(f32)
            prod_hi = prod.astype(bf16)
            prod_lo = (prod - prod_hi.astype(f32)).astype(bf16)
            dsum = (dot_nt(ones, prod_hi) + dot_nt(ones, prod_lo))[:1]

            def branch(c):
                first = REACH - c * 128
                dqt = None
                KB = (1 + c) * QB
                for t in range(1):
                    b = first
                    at = pl.ds(qb * QB + b, KB)
                    s = dot_nt(k_ref[0, at, :], q)
                    dp = dot_nt(v_ref[0, at, :], do)
                    at_first = qb * QB + b
                    rows = lax.broadcasted_iota(jnp.int32, (KB, QB), 0)
                    z = s * LOG2E + (bias_ref[h, pl.ds(b, KB), :] - lse)
                    p = jnp.exp2(jnp.where((rows >= lo - at_first) & (rows <= hi - at_first), z, NEG))
                    ds = (p * (dp - dsum)).astype(bf16)
                    dva_ref[at, :] += dot_nn(p.astype(bf16), do)
                    dka_ref[at, :] += dot_nn(ds, q)
                    part = dot_nn(kt_ref[pl.ds(h * 64, 64), at], ds)
                    dqt = part if t == 0 else dqt + part
                dqt_ref[pl.ds(h * 64, 64), pl.ds(qb * QB, QB)] = dqt * 0.125

            for c in (2, 3, 4):
                pl.when(cls == c)(lambda c=c: branch(c))
    dq_ref[0] = dqt_ref[...].T.astype(bf16)
    dk_ref[0] = dka_ref[...].astype(bf16)
    dv_ref[0] = dva_ref[...].astype(bf16)

def attend_bwd(windows, slopes2, q, kv, do, o, lo, hi, lse):
    seqs, tokens, width = q.shape
    keys = kv.shape[1]
    pairs = width // 128
    smem = pl.BlockSpec(memory_space=pltpu.SMEM)
    tok = pl.BlockSpec((1, tokens, 128), lambda p, s: (s, 0, p))
    key = pl.BlockSpec((1, keys, 128), lambda p, s: (s, 0, p))
    row = pl.BlockSpec((1, 1, tokens), lambda p, s: (s, 0, 0))
    stat = pl.BlockSpec((1, 1, 2, tokens), lambda p, s: (s, p, 0, 0))
    return pl.pallas_call(
        bwd_kernel,
        grid=(pairs, seqs),
        in_specs=[smem, smem, tok, key, pl.BlockSpec((1, keys, 128), lambda p, s: (s, 0, p + pairs)), tok, tok, row, row, stat],
        out_specs=[tok, key, key],
        out_shape=[
            jax.ShapeDtypeStruct((seqs, tokens, width), bf16),
            jax.ShapeDtypeStruct((seqs, keys, width), bf16),
            jax.ShapeDtypeStruct((seqs, keys, width), bf16),
        ],
        scratch_shapes=[
            pltpu.VMEM((128, keys), bf16),
            pltpu.VMEM((128, tokens), f32),
            pltpu.VMEM((keys, 128), f32),
            pltpu.VMEM((keys, 128), f32),
            pltpu.VMEM((2, QB + 2 * REACH, QB), f32),
        ],
        compiler_params=pltpu.CompilerParams(vmem_limit_bytes=40 * 2**20),
        cost_estimate=pl.CostEstimate(flops=5 * 10**10, bytes_accessed=2 * 10**7, transcendentals=10**7),
        name="attend_bwd",
    )(windows, slopes2, q, kv, kv, do, o, lo, hi, lse)

def shifted(value, axis, by):
    peers = lax.axis_size(axis)
    pairs = [(i, i + by) for i in range(peers) if 0 <= i + by < peers]
    return lax.ppermute(value, axis, pairs)


def swapped(value, axis, bit):
    peers = lax.axis_size(axis)
    return lax.ppermute(value, axis, [(i, i ^ bit) for i in range(peers)])


def layer_norm(rows_in):
    center = rows_in - jnp.mean(rows_in, axis=-1, keepdims=True)
    spread = jnp.mean(center * center, axis=-1, keepdims=True)
    scale = lax.rsqrt(spread + 1e-05)
    return center * scale, scale


def layer_norm_back(grad, hat, scale, gain):
    inner = grad * gain
    mean_one = jnp.mean(inner, axis=-1, keepdims=True)
    mean_two = jnp.mean(inner * hat, axis=-1, keepdims=True)
    back = scale * (inner - mean_one - hat * mean_two)
    return back, jnp.sum(grad * hat, axis=0, keepdims=True), jnp.sum(grad, axis=0, keepdims=True)


def exchange(small, keep, give, axis, bit, beside=()):
    high = small.astype(bf16)
    both = jnp.concatenate([high, (small - high.astype(f32)).astype(bf16)])
    lead, cols = give.shape[:-2], give.shape[-1]
    flat = give.reshape(-1, cols)
    tail = jnp.pad(both, ((0, 0), (0, cols - both.shape[1])))
    got = swapped(jnp.concatenate([flat, tail]), axis, bit)
    if beside:
        got, beside = lax.optimization_barrier((got, beside))
    terms = got[flat.shape[0] :, : both.shape[1]].astype(f32)
    theirs = terms[:8] + terms[8:]
    ours = both[:8].astype(f32) + both[8:].astype(f32)
    is_peak_row = lax.broadcasted_iota(jnp.int32, (8, 1), 0) == 4
    small = jnp.where(is_peak_row, jnp.maximum(ours, theirs), ours + theirs)
    total = (keep.astype(f32) + got[: flat.shape[0]].reshape(give.shape).astype(f32)).astype(bf16)
    return (small, total, *beside)


def halve(small, value, axis, bit):
    side = (lax.axis_index(axis) // bit) % 2
    keep = lax.dynamic_index_in_dim(value, side, 1, False)
    return exchange(small, keep, lax.dynamic_index_in_dim(value, 1 - side, 1, False), axis, bit)


def pick_units(slot_of, sources, count, pad=0):
    slots, rows, width = sources[0].shape

    def kernel(slot_ref, *refs):
        out_ref = refs[-1]
        if pad:
            out_ref[:, pl.ds(count * width, pad)] = jnp.zeros((rows, pad), out_ref.dtype)
        for u in range(count):
            at = pl.ds(u * width, width)
            for number, ref in enumerate(refs[:-1]):

                @pl.when(slot_ref[0, u] == number)
                def _(ref=ref, u=u, at=at):
                    out_ref[:, at] = ref[slot_ref[1, u]]

    vmem = pl.BlockSpec(memory_space=pltpu.VMEM)
    return pl.pallas_call(
        kernel,
        in_specs=[pl.BlockSpec(memory_space=pltpu.SMEM)] + [vmem] * len(sources),
        out_specs=vmem,
        out_shape=jax.ShapeDtypeStruct((rows, count * width + pad), sources[0].dtype),
        compiler_params=pltpu.CompilerParams(vmem_limit_bytes=24 * 2**20),
        name="pick_units",
    )(slot_of, *sources)


def to_slots(unit_of, columns, slots, width):
    rows = columns.shape[0]

    def kernel(unit_ref, col_ref, out_ref):
        for s in range(slots):
            unit = unit_ref[s]

            @pl.when(unit >= 0)
            def _(s=s, unit=unit):
                out_ref[s] = col_ref[:, pl.ds(pl.multiple_of(unit * width, 128), width)]

            @pl.when(unit < 0)
            def _(s=s):
                out_ref[s] = jnp.zeros((rows, width), out_ref.dtype)

    vmem = pl.BlockSpec(memory_space=pltpu.VMEM)
    return pl.pallas_call(
        kernel,
        in_specs=[pl.BlockSpec(memory_space=pltpu.SMEM), vmem],
        out_specs=vmem,
        out_shape=jax.ShapeDtypeStruct((slots, rows, width), columns.dtype),
        compiler_params=pltpu.CompilerParams(vmem_limit_bytes=24 * 2**20),
        name="to_slots",
    )(unit_of, columns)


def adam_slots(unit_of, weights, first, second, grads, scale, correction, rate):
    slots, rows, width = weights.shape

    def kernel(unit_ref, w_ref, m_ref, v_ref, scale_ref, *refs):
        grad_refs, (g_out, w_out, m_out, v_out, low_out) = refs[:-5], refs[-5:]
        unit = unit_ref[pl.program_id(0)]
        live = unit >= 0
        g = grad_refs[0][0].astype(f32)
        for ref in grad_refs[1:]:
            g = g + ref[0].astype(f32)
        g = jnp.where(live, g, 0.0)
        w = w_ref[0]
        m = 0.5 * m_ref[0] + 0.5 * g
        v = 0.5 * v_ref[0] + 0.5 * g * g
        step = m * (1.0 / correction) / (jnp.sqrt(v * (1.0 / correction)) + 1e-08)
        moved = w - rate * (step + decay_rate * w)
        moved = jnp.where((unit == 0) | (unit == 1), moved * scale_ref[...], moved)
        moved = jnp.where(live, moved, 0.0)
        g_out[0] = g
        w_out[0] = moved
        m_out[0] = jnp.where(live, m, 0.0)
        v_out[0] = jnp.where(live, v, 0.0)
        low_out[0] = moved.astype(bf16)

    block = pl.BlockSpec((1, rows, width), lambda s: (s, 0, 0))
    wide = jax.ShapeDtypeStruct(weights.shape, f32)
    return pl.pallas_call(
        kernel,
        grid=(slots,),
        in_specs=[pl.BlockSpec(memory_space=pltpu.SMEM), block, block, block,
                  pl.BlockSpec((1, width), lambda s: (0, 0))] + [block] * len(grads),
        out_specs=[block] * 5,
        out_shape=[wide] * 4 + [jax.ShapeDtypeStruct(weights.shape, bf16)],
        compiler_params=pltpu.CompilerParams(vmem_limit_bytes=24 * 2**20),
        name="adam_slots",
    )(unit_of, weights, first, second, scale, *grads)


def adam_step(master, gradient, first, second, correction, learn_rate):
    new_first = 0.5 * first + 0.5 * gradient
    new_second = 0.5 * second + 0.5 * gradient * gradient
    normed = new_first / correction / (jnp.sqrt(new_second / correction) + 1e-08)
    return (master - learn_rate * (normed + decay_rate * master), new_first, new_second)


def dot_tn(a, b):
    return lax.dot_general(a, b, (((0,), (0,)), ((), ())), preferred_element_type=f32)


def gelu_parts(gate):
    cdf = 0.5 * (1.0 + lax.erf(gate * 0.7071067811865476))
    density = 0.3989422804014327 * jnp.exp(-0.5 * gate * gate)
    return cdf, density


RB = 512
CHUNK = 256


def ffn_kernel(o_ref, x_ref, og_ref, wo_ref, wg_ref, wu_ref, wd_ref, norm_ref,
               out_ref, first_ref, ograd_ref, small_ref, grads_ref,
               hat_ref, scale_ref, acc_ref, a_ref, b_ref, h_ref, ylow_ref, ylowt_ref, fgrad_ref,
               gg_ref, ug_ref, stage_g, stage_u, stage_d, stage_o, sems):
    step = pl.program_id(0)
    rows, width = x_ref.shape
    chunk = wg_ref.shape[1]
    chunks = FF // chunk
    blocks = rows // RB

    def at(i):
        return pl.ds(i * RB, RB)

    def copies(j):
        slot = lax.rem(j, 2)
        column = pl.multiple_of(width + j * chunk, 128)
        per = width // chunk
        return (
            pltpu.make_async_copy(stage_g.at[slot], grads_ref.at[:, pl.ds(column, chunk)], sems.at[slot, 0]),
            pltpu.make_async_copy(stage_u.at[slot], grads_ref.at[:, pl.ds(column + FF, chunk)], sems.at[slot, 1]),
            pltpu.make_async_copy(
                stage_d.at[slot],
                grads_ref.at[pl.ds(pl.multiple_of(lax.rem(j, per) * chunk, 128), chunk),
                             pl.ds(pl.multiple_of(width + 2 * FF + lax.div(j, per) * width, 128), width)],
                sems.at[slot, 2],
            ),
        )

    @pl.when(step == 0)
    def _():
        for i in range(blocks):
            total = x_ref[at(i), :].astype(f32) + dot_nn(o_ref[at(i), :], wo_ref[...])
            hat, scale = layer_norm(total)
            y1 = hat * norm_ref[0:1, :] + norm_ref[1:2, :]
            hat_ref[at(i), :] = hat
            scale_ref[at(i), :] = scale
            acc_ref[at(i), :] = y1
            ylow_ref[at(i), :] = y1.astype(bf16)
            ylowt_ref[:, at(i)] = y1.T.astype(bf16)

    @pl.when(step < chunks)
    def _():
        for i in range(blocks):
            y = ylow_ref[at(i), :]
            gate = dot_nn(y, wg_ref[...])
            up = dot_nn(y, wu_ref[...])
            cdf, density = gelu_parts(gate)
            a = gate * cdf
            hidden = (a * up).astype(bf16)
            a_ref[step, at(i), :] = a.astype(bf16)
            b_ref[step, at(i), :] = (up * (cdf + gate * density)).astype(bf16)
            h_ref[step, at(i), :] = hidden
            acc_ref[at(i), :] += dot_nn(hidden, wd_ref[...])

    @pl.when(step == chunks)
    def _():
        gain = bias = None
        for i in range(blocks):
            hat, scale = layer_norm(acc_ref[at(i), :])
            out_ref[at(i), :] = (hat * norm_ref[2:3, :] + norm_ref[3:4, :]).astype(bf16)
            grad = og_ref[at(i), :].astype(f32)
            back, g, b = layer_norm_back(grad, hat, scale, norm_ref[2:3, :])
            gain = g if i == 0 else gain + g
            bias = b if i == 0 else bias + b
            acc_ref[at(i), :] = back
            fgrad_ref[at(i), :] = back.astype(bf16)
        small_ref[2:3, :] = gain
        small_ref[3:4, :] = bias

    @pl.when(step >= chunks)
    def _():
        j = step - chunks
        slot = lax.rem(j, 2)

        @pl.when(j >= 2)
        def _():
            for copy in copies(j - 2):
                copy.wait()

        for i in range(blocks):
            hidden_grad = dot_nt(fgrad_ref[at(i), :], wd_ref[...])
            gg = (hidden_grad * b_ref[j, at(i), :].astype(f32)).astype(bf16)
            ug = (hidden_grad * a_ref[j, at(i), :].astype(f32)).astype(bf16)
            gg_ref[at(i), :] = gg
            ug_ref[at(i), :] = ug
            acc_ref[at(i), :] += dot_nt(gg, wg_ref[...]) + dot_nt(ug, wu_ref[...])
        stage_g[slot] = dot_nn(ylowt_ref[...], gg_ref[...]).astype(bf16)
        stage_u[slot] = dot_nn(ylowt_ref[...], ug_ref[...]).astype(bf16)
        stage_d[slot] = dot_tn(h_ref[j], fgrad_ref[...]).astype(bf16)
        for copy in copies(j):
            copy.start()

    @pl.when(step == 2 * chunks - 1)
    def _():
        gain = bias = None
        for i in range(blocks):
            back, g, b = layer_norm_back(acc_ref[at(i), :], hat_ref[at(i), :], scale_ref[at(i), :], norm_ref[0:1, :])
            gain = g if i == 0 else gain + g
            bias = b if i == 0 else bias + b
            first_ref[at(i), :] = back
            low = back.astype(bf16)
            fgrad_ref[at(i), :] = low
            ograd_ref[at(i), :] = dot_nt(low, wo_ref[...]).astype(bf16)
        small_ref[0:1, :] = gain
        small_ref[1:2, :] = bias
        small_ref[4:8, :] = jnp.zeros((4, width), f32)
        stage_o[...] = dot_tn(o_ref[...], fgrad_ref[...]).astype(bf16)
        last = pltpu.make_async_copy(stage_o, grads_ref.at[:, pl.ds(0, width)], sems.at[2, 0])
        last.start()
        for j in (chunks - 2, chunks - 1):
            for copy in copies(j):
                copy.wait()
        last.wait()


def feed_forward(o, x, out_grad, w_rest, norms):
    rows, width = x.shape
    chunks = FF // CHUNK
    lead = width // CHUNK
    per = width // CHUNK

    def whole(shape):
        return pl.BlockSpec(shape, lambda s: (0,) * len(shape), pipeline_mode=pl.Buffered(1))

    full = whole((rows, width))
    return pl.pallas_call(
        ffn_kernel,
        grid=(2 * chunks,),
        in_specs=[
            full, full, full,
            whole((width, width)),
            pl.BlockSpec((width, CHUNK), lambda s: (0, lead + lax.rem(s, chunks))),
            pl.BlockSpec((width, CHUNK), lambda s: (0, lead + chunks + lax.rem(s, chunks))),
            pl.BlockSpec((CHUNK, width), lambda s: (lax.rem(lax.rem(s, chunks), per), 1 + 2 * FF // width + lax.div(lax.rem(s, chunks), per))),
            whole(norms.shape),
        ],
        out_specs=[full, full, full, whole((8, width)), pl.BlockSpec(memory_space=pl.ANY)],
        out_shape=[
            jax.ShapeDtypeStruct((rows, width), bf16),
            jax.ShapeDtypeStruct((rows, width), f32),
            jax.ShapeDtypeStruct((rows, width), bf16),
            jax.ShapeDtypeStruct((8, width), f32),
            jax.ShapeDtypeStruct((width, width + 3 * FF), bf16),
        ],
        scratch_shapes=[
            pltpu.VMEM((rows, width), f32),
            pltpu.VMEM((rows, 1), f32),
            pltpu.VMEM((rows, width), f32),
            pltpu.VMEM((chunks, rows, CHUNK), bf16),
            pltpu.VMEM((chunks, rows, CHUNK), bf16),
            pltpu.VMEM((chunks, rows, CHUNK), bf16),
            pltpu.VMEM((rows, width), bf16),
            pltpu.VMEM((width, rows), bf16),
            pltpu.VMEM((rows, width), bf16),
            pltpu.VMEM((rows, CHUNK), bf16),
            pltpu.VMEM((rows, CHUNK), bf16),
            pltpu.VMEM((2, width, CHUNK), bf16),
            pltpu.VMEM((2, width, CHUNK), bf16),
            pltpu.VMEM((2, CHUNK, width), bf16),
            pltpu.VMEM((width, width), bf16),
            pltpu.SemaphoreType.DMA((3, 3)),
        ],
        compiler_params=pltpu.CompilerParams(vmem_limit_bytes=58 * 2**20),
        cost_estimate=pl.CostEstimate(flops=46 * 10**9, bytes_accessed=6 * 10**7, transcendentals=6 * 10**6),
        name="feed_forward",
    )(o, x, out_grad, w_rest, w_rest, w_rest, w_rest, norms)

def first_gradients(x_t, dq, dk, dv, tokens):
    width, total = x_t.shape
    seqs = dq.shape[0] // tokens
    keys = total // seqs
    cols = 256
    per = width // cols

    def kernel(x_ref, q_ref, k_ref, v_ref, out_ref):
        unit = pl.program_id(0)

        @pl.when(unit == 0)
        def _():
            acc = None
            for s in range(seqs):
                part = dot_nn(x_ref[:, pl.ds(s * keys + REACH, tokens)], q_ref[pl.ds(s * tokens, tokens), :])
                acc = part if s == 0 else acc + part
            out_ref[...] = acc.astype(bf16)

        @pl.when(unit == 1)
        def _():
            out_ref[...] = dot_nn(x_ref[...], k_ref[...]).astype(bf16)

        @pl.when(unit == 2)
        def _():
            out_ref[...] = dot_nn(x_ref[...], v_ref[...]).astype(bf16)

    return pl.pallas_call(
        kernel,
        grid=(3, per),
        in_specs=[
            pl.BlockSpec((width, total), lambda u, c: (0, 0), pipeline_mode=pl.Buffered(1)),
            pl.BlockSpec((dq.shape[0], cols), lambda u, c: (0, jnp.where(u == 0, c, per - 1))),
            pl.BlockSpec((total, cols), lambda u, c: (0, jnp.where(u == 0, 0, jnp.where(u == 1, c, per - 1)))),
            pl.BlockSpec((total, cols), lambda u, c: (0, jnp.where(u == 2, c, 0))),
        ],
        out_specs=pl.BlockSpec((width, cols), lambda u, c: (0, u * per + c)),
        out_shape=jax.ShapeDtypeStruct((width, 3 * width), bf16),
        compiler_params=pltpu.CompilerParams(vmem_limit_bytes=32 * 2**20),
        cost_estimate=pl.CostEstimate(flops=9 * 10**9, bytes_accessed=2 * 10**7, transcendentals=0),
        name="first_gradients",
    )(x_t, dq, dk, dv)


def input_parts(first_grad, dq, dk, dv, w_first):
    seqs, tokens, width = dq.shape
    keys = dk.shape[1]
    pieces = REACH // tokens

    def kernel(first_ref, q_ref, k_ref, v_ref, w_ref, own_ref, rim_ref):
        block = pl.program_id(1)
        part = dot_nt(k_ref[0], w_ref[:, width : 2 * width]) + dot_nt(v_ref[0], w_ref[:, 2 * width :])

        @pl.when(block == pieces)
        def _():
            own_ref[0] = first_ref[0] + part + dot_nt(q_ref[0], w_ref[:, :width])

        @pl.when(block != pieces)
        def _():
            rim_ref[0, 0] = part.astype(bf16)

    own = pl.BlockSpec((1, tokens, width), lambda s, b: (s, 0, 0))
    key = pl.BlockSpec((1, tokens, width), lambda s, b: (s, b, 0))
    return pl.pallas_call(
        kernel,
        grid=(seqs, keys // tokens),
        in_specs=[own, own, key, key,
                  pl.BlockSpec(w_first.shape, lambda s, b: (0, 0), pipeline_mode=pl.Buffered(1))],
        out_specs=[own, pl.BlockSpec((1, 1, tokens, width), lambda s, b: (s, jnp.where(b < pieces, b, jnp.maximum(b - 1, 0)), 0, 0))],
        out_shape=[
            jax.ShapeDtypeStruct((seqs, tokens, width), f32),
            jax.ShapeDtypeStruct((seqs, 2 * pieces, tokens, width), bf16),
        ],
        compiler_params=pltpu.CompilerParams(vmem_limit_bytes=32 * 2**20),
        cost_estimate=pl.CostEstimate(flops=9 * 10**9, bytes_accessed=2 * 10**7, transcendentals=0),
        name="input_parts",
    )(first_grad, dq, dk, dv, w_first)


def on_device(inputs, out_grad, segments, windows, owners, weights, first_moments, second_moments,
              norm_params, norm_first, norm_second):
    seqs, tokens, width = inputs.shape
    rows = seqs * tokens
    heads = windows.shape[0]
    slots = weights.shape[0]
    owner_count = lax.axis_size("seq")
    me = lax.axis_index("seq")
    seq_len = segments.shape[1]
    keys = tokens + 2 * REACH
    pieces = REACH // tokens
    groups = FF // width
    units = owners.shape[0]
    rest = units - 3
    row_count = weights.shape[1]

    ids = jnp.arange(units, dtype=jnp.int32)
    before = (owners[None, :] == owners[:, None]) & (ids[None, :] < ids[:, None])
    rank = jnp.sum(before.astype(jnp.int32), axis=1)
    slot_ids = jnp.arange(owner_count * slots, dtype=jnp.int32)
    match = (owners * slots + rank)[None, :] == slot_ids[:, None]
    unit_of = jnp.max(jnp.where(match, ids[None, :], -1), axis=1)
    my_units = lax.dynamic_slice_in_dim(unit_of, me * slots, slots, 0)

    left = [shifted(inputs, "ctx", pieces - n) for n in range(pieces)]
    right = [shifted(inputs, "ctx", -(n + 1)) for n in range(pieces)]

    low = weights.astype(bf16)
    if owner_count == 2:
        place = jnp.stack([jnp.where(owners == me, 0, 1), rank])
        own_first = pick_units(place[:, :3] * jnp.array([[0], [1]], jnp.int32), [low], 3)
        got_first = swapped(own_first, "seq", 1)
        mine = jnp.repeat(owners[:3] == me, width)[None, :]
        picked_first = jnp.where(mine, own_first, got_first)
        sources = [low, swapped(low, "seq", 1)]
    else:
        every = lax.all_gather(low, "seq", axis=0, tiled=True)
        place = jnp.stack([jnp.zeros_like(owners), owners * slots + rank])
        sources = [every]
        picked_first = pick_units(place[:, :3], sources, 3)
    w_first = lax.all_gather(picked_first, "ctx", axis=0, tiled=True)
    picked_rest = pick_units(place[:, 3:], sources, rest, 1024)
    picked_rest, w_first, left, right = lax.optimization_barrier((picked_rest, w_first, left, right))
    w_rest = lax.all_gather(picked_rest, "ctx", axis=0, tiled=True)

    start = lax.axis_index("ctx") * tokens
    padded = jnp.pad(segments, ((0, 0), (REACH, 0)), constant_values=-1)
    padded = jnp.pad(padded, ((0, 0), (0, REACH)), constant_values=1 << 20)
    key_seg = lax.dynamic_slice_in_dim(padded, start, keys, 1)
    query_seg = key_seg[:, REACH : REACH + tokens]
    lo = jnp.sum((key_seg[:, :, None] < query_seg[:, None, :]).astype(jnp.int32), axis=1)[:, None]
    hi = jnp.sum((key_seg[:, :, None] <= query_seg[:, None, :]).astype(jnp.int32), axis=1)[:, None] - 1
    slopes2 = jnp.power(2.0, -8.0 * (jnp.arange(heads, dtype=f32) + 1.0) / heads) * LOG2E

    x_ext = jnp.concatenate(left + [inputs] + right, axis=1)
    ctx = lax.axis_index("ctx")
    by_core = jnp.transpose(x_ext.reshape(seqs * keys, width)).reshape(width // (2 * row_count), 2, row_count, seqs * keys)
    x_t = jnp.concatenate([lax.dynamic_index_in_dim(by_core, ctx % 2, 1, False), lax.dynamic_index_in_dim(by_core, 1 - ctx % 2, 1, False)])
    x_t = x_t.reshape(width, seqs * keys)
    w_q, w_kv = w_first[:, :width], w_first[:, width:]
    x = inputs.reshape(rows, width)
    q = dot_nn(x, w_q).astype(bf16).reshape(seqs, tokens, width)
    kv = dot_nn(x_ext.reshape(seqs * keys, width), w_kv).astype(bf16).reshape(seqs, keys, 2 * width)
    mixed, lse, peaks = attend_fwd(windows, slopes2, q, kv, lo, hi)
    peak = jnp.max(peaks, axis=(1, 2))
    o = mixed.reshape(rows, width)

    x_t, w_rest = lax.optimization_barrier((x_t, w_rest))
    result, first_grad, o_grad, small, rest_grads = feed_forward(
        o, x, out_grad.reshape(rows, width), w_rest, norm_params
    )
    output = result.reshape(seqs, tokens, width)
    rest_sums = lax.psum_scatter(rest_grads, "ctx", scatter_dimension=0, tiled=True)
    dq, dk, dv = attend_bwd(windows, slopes2, q, kv, o_grad.reshape(seqs, tokens, width), mixed, lo, hi, lse)

    def owned_pair(columns, lowest):
        local = unit_of - lowest
        local = jnp.where((local >= 0) & (local < columns.shape[1] // width), local, -1)
        if owner_count == 2:
            ours = lax.dynamic_slice_in_dim(local, me * slots, slots, 0)
            theirs = lax.dynamic_slice_in_dim(local, (1 - me) * slots, slots, 0)
            return to_slots(ours, columns, slots, width), to_slots(theirs, columns, slots, width)
        return None, to_slots(local, columns, owner_count * slots, width)

    input_grad, rim = input_parts(first_grad.reshape(seqs, tokens, width), dq, dk, dv, w_first)

    is_peak_row = (jnp.arange(8) == 4)[:, None]
    small = jnp.where(is_peak_row, jnp.pad(peak, (0, width - heads))[None], small)
    first_grads = first_gradients(
        x_t, dq.reshape(rows, width), dk.reshape(seqs * keys, width), dv.reshape(seqs * keys, width), tokens
    )
    half = width // 2
    small, value = exchange(small, first_grads[:half], first_grads[half:], "ctx", 1)
    if owner_count == 2:
        columns = 3 * width // 2
        small, value, input_grad, rim = exchange(
            small,
            lax.dynamic_slice_in_dim(value, me * columns, columns, 1),
            lax.dynamic_slice_in_dim(value, (1 - me) * columns, columns, 1),
            "seq", 1, (input_grad, rim),
        )
    value = value.reshape(-1, row_count, value.shape[1])
    keep, give = owned_pair(rest_sums, 3)
    bit = 2
    arrived = []
    while bit < lax.axis_size("ctx"):
        if 2 * bit == lax.axis_size("ctx"):
            value, _ = lax.optimization_barrier((value, give))
        small, value = halve(small, value.reshape((-1, 2) + value.shape[1:]), "ctx", bit)
        if bit == 2:
            for n in range(pieces):
                arrived += [shifted(rim[:, n], "ctx", n - pieces), shifted(rim[:, pieces + n], "ctx", n + 1)]
        bit *= 2
    first_sums = value[0]
    bit = 1
    while owner_count != 2 and bit < owner_count:
        other = swapped(small, "seq", bit)
        small = jnp.where(is_peak_row, jnp.maximum(small, other), small + other)
        bit *= 2
    norm_grads = small[:4]
    factors = clip_level / jnp.maximum(small[4, :heads], clip_level)
    column_scale = jnp.repeat(jnp.sqrt(factors), width // heads)[None, :]
    correction = 1.0 - 0.5**STEP

    if owner_count == 2:
        other = swapped(first_sums, "seq", 1)
        other, arrived = lax.optimization_barrier((other, arrived))
        whole = jnp.concatenate([jnp.where(me == 0, first_sums, other), jnp.where(me == 0, other, first_sums)], axis=1)
        parts = [keep, swapped(give, "seq", 1), to_slots(jnp.where(my_units < 3, my_units, -1), whole, slots, width)]
    else:
        parts = [lax.psum_scatter(give, "seq", scatter_dimension=0, tiled=True),
                 lax.psum_scatter(owned_pair(first_sums, 0)[1], "seq", scatter_dimension=0, tiled=True)]
    weight_grads, new_weights, new_first, new_second, weights_low = adam_slots(
        my_units, weights, first_moments, second_moments, parts, column_scale, correction, 0.5 / D**0.5
    )
    for piece in arrived:
        input_grad = input_grad + piece.astype(f32)
    new_norms, new_norm_first, new_norm_second = adam_step(
        norm_params, norm_grads, norm_first, norm_second, correction, norm_rate
    )
    return (output, input_grad, weight_grads, norm_grads, new_weights, new_first, new_second, weights_low,
            new_norms, new_norm_first, new_norm_second, factors)


def solution(mesh):
    block = P("seq", "ctx", None)
    return jax.shard_map(
        on_device,
        mesh=mesh,
        in_specs=(block, block, P("seq", None), P(), P(), block, block, block, P(), P(), P()),
        out_specs=(block, block, block, P(), block, block, block, block, P(), P(), P(), P()),
        check_vma=False,
    )
```
